32 devices in a mesh: gx: 2 (over y), gy: 4 (over z), pa: 4 (over x, core).
Axes of the slice: x: 2, y: 2, z: 4, core: 2. Of those that a mesh axis runs over, the one named last changes fastest.
Arguments:
- latents: bfloat16 [32, 128, 768], P(('gx', 'pa'), 'gy'), may hold values from -6 to 6
- noise: bfloat16 [2, 32, 128, 768], P(None, ('gx', 'pa'), 'gy'), may hold values from -6 to 6
- proc_gain: float32 [768], replicated, may hold values from 0.1 to 1.9
- w_qkv: bfloat16 [768, 2304], P(('gx', 'pa')), may hold values from -0.21875 to 0.21875
- w_out: bfloat16 [768, 768], P(('gx', 'pa')), may hold values from -0.21875 to 0.21875
- w_query: bfloat16 [128, 768], P(('gx', 'pa')), may hold values from -0.5 to 0.5
- w_head: bfloat16 [768, 3], P(('gx', 'pa')), may hold values from -0.21875 to 0.21875
- probe_cell: int32 [32768], P(('gx', 'gy', 'pa')), may hold values from 0 to 127
- probe_offset: float32 [2, 32768], P(None, ('gx', 'gy', 'pa')), may hold values from 0 to 1
- probe_count: int32 [32], P(('gx', 'gy', 'pa')), may hold values from 128 to 1024, as said below
Outputs:
- latent_out: bfloat16 [32, 128, 768], P(('gx', 'pa'), 'gy')
- probe_values: float32 [3, 32768], P(None, ('gx', 'gy', 'pa'))
The draws below stay inside these ranges and needn't reach their ends.
Inputs may be any that keep to these rules, and one draw needn't show every extreme that they name: `probe_cell`: a cell of the device's own 4 x 32 block, numbered row by row. `probe_count`: slots below the count hold probes, the others are empty; in every draw one device has all 1024 slots live.
All inputs are finite; a program needn't handle non-finite values.
Results may differ from the reference program's by a relative error of at most 0.02.
Values may be sent and summed in bfloat16 or wider, within the bound.
A program may use at most 64 MiB of HBM per device.

```python
import math
import jax
import jax.numpy as jnp
from jax import lax

D = 768
HEADS = 12
FQ = 128
CH = 3
RAD = 3
STEPS = 2
ROWS = 4
COLS = 32
PCAP = 1024
LX = 32
LY = 128
NPROBE = 32768
N_GY = 4
N_PA = 4


def draw_probe_count(key, part):
    device_total = NPROBE // PCAP
    first, second, third = jax.random.split(jax.random.fold_in(key, 11), 3)
    counts = jax.random.randint(first, (device_total,), PCAP // 8, PCAP + 1)
    fullest = jax.random.randint(second, (), 0, device_total)
    sparse = (fullest + 1 + jax.random.randint(third, (), 0, device_total - 1)) % device_total
    places = jnp.arange(device_total, dtype=jnp.int32)
    counts = jnp.where(places == sparse, PCAP // 8, counts)
    counts = jnp.where(places == fullest, PCAP, counts)
    return counts.astype(jnp.int32)


def touch_ends(array, own_key, low, top_value):
    longest = array.shape.index(max(array.shape))
    spots = []
    for shift in (0, 1):
        where = [jax.random.randint(jax.random.fold_in(own_key, axis), (), 0, length) for axis, length in enumerate(array.shape)]
        where[longest] = (where[longest] + shift) % array.shape[longest]
        spots.append(tuple(where))
    return array.at[spots[0]].set(low).at[spots[1]].set(top_value)


def level_of(key, extent, cuts, smallest, top_value):
    loudness, own = 1.0, jax.random.fold_in(key, 6)
    for dim, parts in cuts:
        steps = jnp.exp(jax.random.uniform(jax.random.fold_in(own, dim), (parts,), jnp.float32, smallest / len(cuts), top_value / len(cuts)))
        loudness = loudness * jnp.repeat(steps, extent[dim] // parts).reshape([-1 if axis == dim else 1 for axis in range(len(extent))])
    return loudness


def bell_draw(key, dims, deviation, bound, pieces=(), held_as=jnp.bfloat16):
    gain = level_of(key, dims, pieces, -0.22, 0.18) if pieces else 1.0
    drawn = jax.random.normal(key, dims, jnp.float32) * deviation * gain
    return jnp.minimum(jnp.maximum(drawn, -bound), bound).astype(held_as)


def setup_inputs(seed: int = 0) -> dict:
    streams_of = jax.random.split(jax.random.key(seed), 11)
    return {
        "latents": bell_draw(streams_of[0], (LX, LY, D), 1.0, 6.0, ((0, 8), (1, 4))),
        "noise": bell_draw(streams_of[1], (STEPS, LX, LY, D), 1.0, 6.0, ((1, 8), (2, 4))),
        "proc_gain": jnp.clip(1.0 + 0.18 * jax.random.normal(streams_of[2], (D,), jnp.float32), 0.1, 1.9),
        "w_qkv": bell_draw(streams_of[3], (D, 3 * D), D ** -0.5, 0.21875, ((0, 8),)),
        "w_out": bell_draw(streams_of[4], (D, D), D ** -0.5, 0.21875, ((0, 8),)),
        "w_query": bell_draw(streams_of[5], (FQ, D), FQ ** -0.5, 0.5, ((0, 8),)),
        "w_head": bell_draw(streams_of[6], (D, CH), D ** -0.5, 0.21875, ((0, 8),)),
        "probe_cell": touch_ends(jax.random.randint(streams_of[7], (NPROBE,), 0, ROWS * COLS), jax.random.fold_in(streams_of[7], 1), 0, (ROWS * COLS) - 1).astype(jnp.int32),
        "probe_offset": jnp.clip(1.0 * jax.random.uniform(streams_of[8], (2, NPROBE), jnp.float32) ** level_of(streams_of[8], (2, NPROBE), ((1, 32),), -0.2, 0.2), 0.0, 1.0),
        "probe_count": draw_probe_count(jax.random.fold_in(streams_of[10], 71), 0),
    }


EPS = 1e-06
NOISE_COEF = 0.3

def normalize(tokens, gain_vec):
    values = tokens.astype(jnp.float32)
    factor = lax.rsqrt(lax.optimization_barrier(jnp.mean(values * values, axis=-1, keepdims=True)) + EPS)
    return (values * factor * gain_vec.astype(jnp.float32)).astype(jnp.bfloat16)

def neighbour_attention(queries, key_values, row_count, col_count):
    model_width = queries.shape[-1]
    head_size = model_width // HEADS
    window_span = 2 * RAD + 1
    query_four = queries.astype(jnp.float32).reshape(row_count, col_count, HEADS, head_size)
    score_list = []
    for row_step in range(window_span):
        for col_step in range(window_span):
            key_rows = key_values[row_step:row_step + row_count, col_step:col_step + col_count, :model_width]
            key_four = key_rows.astype(jnp.float32).reshape(row_count, col_count, HEADS, head_size)
            score_list.append(jnp.einsum('rchd,rchd->rch', query_four, key_four) / math.sqrt(head_size))
    scores = jnp.stack(score_list)
    weights = jax.nn.softmax(scores, axis=0).astype(jnp.bfloat16)
    summed = jnp.zeros((row_count, col_count, HEADS, head_size), jnp.float32)
    for row_step in range(window_span):
        for col_step in range(window_span):
            value_rows = key_values[row_step:row_step + row_count, col_step:col_step + col_count, model_width:]
            value_four = value_rows.astype(jnp.float32).reshape(row_count, col_count, HEADS, head_size)
            weight_now = weights[row_step * window_span + col_step].astype(jnp.float32)
            summed = summed + weight_now[..., None] * value_four
    return summed.reshape(row_count, col_count, model_width).astype(jnp.bfloat16)

def wrap_extend(grid, depth):
    grid = jnp.concatenate([grid[-depth:], grid, grid[:depth]], axis=0)
    return jnp.concatenate([grid[:, -depth:], grid, grid[:, :depth]], axis=1)

def decode_block(context, offsets, w_query, w_head):
    block_size = context.shape[0]
    model_width = context.shape[-1]
    head_size = model_width // HEADS
    freq = jnp.arange(1, FQ // 4 + 1, dtype=jnp.float32)
    angle_x = 2.0 * math.pi * offsets[0][:, None] * freq[None, :]
    angle_y = 2.0 * math.pi * offsets[1][:, None] * freq[None, :]
    features = jnp.concatenate([jnp.sin(angle_x), jnp.cos(angle_x), jnp.sin(angle_y), jnp.cos(angle_y)], axis=1).astype(jnp.bfloat16)
    probe_query = jnp.dot(features, w_query, preferred_element_type=jnp.float32).astype(jnp.bfloat16)
    query_three = probe_query.astype(jnp.float32).reshape(block_size, HEADS, head_size)
    context_four = context.astype(jnp.float32).reshape(block_size, 9, HEADS, head_size)
    scores = jnp.einsum('phd,pmhd->pmh', query_three, context_four) / math.sqrt(head_size)
    weights = jax.nn.softmax(scores, axis=1).astype(jnp.bfloat16)
    mixed = jnp.einsum('pmh,pmhd->phd', weights.astype(jnp.float32), context_four)
    mixed = mixed.reshape(block_size, model_width).astype(jnp.bfloat16)
    return jnp.dot(mixed, w_head, preferred_element_type=jnp.float32)

def reference(latents, noise, proc_gain, w_qkv, w_out, w_query, w_head, probe_cell, probe_offset, probe_count):
    grid_rows, grid_cols, model_width = latents.shape
    latent = latents
    for step in range(STEPS):
        normed = normalize(latent, proc_gain)
        triple = lax.map(lambda row_tokens: jnp.dot(row_tokens, w_qkv, preferred_element_type=jnp.float32).astype(jnp.bfloat16), normed)
        queries = triple[..., :model_width]
        key_values = wrap_extend(triple[..., model_width:], RAD)

        def one_row(index):
            rows_in = lax.dynamic_slice_in_dim(key_values, index, 2 * RAD + 1, 0)
            row_query = lax.dynamic_slice_in_dim(queries, index, 1, 0)
            attended = neighbour_attention(row_query, rows_in, 1, grid_cols)
            return jnp.dot(attended[0], w_out, preferred_element_type=jnp.float32)
        updates = lax.map(one_row, jnp.arange(grid_rows, dtype=jnp.int32))
        latent = (latent.astype(jnp.float32) + updates / STEPS + NOISE_COEF * noise[step].astype(jnp.float32)).astype(jnp.bfloat16)
    final_ext = wrap_extend(latent, 1)
    flat_ext = final_ext.reshape(-1, model_width)
    slots = jnp.arange(NPROBE, dtype=jnp.int32)
    device = slots // PCAP
    pa_index = device % N_PA
    gy_index = device // N_PA % N_GY
    gx_index = device // (N_PA * N_GY)
    grid_row = (gx_index * N_PA + pa_index) * ROWS + probe_cell // COLS
    grid_col = gy_index * COLS + probe_cell % COLS
    index_list = []
    for row_step in range(3):
        for col_step in range(3):
            index_list.append((grid_row + row_step) * (grid_cols + 2) + grid_col + col_step)
    cell_index = jnp.stack(index_list, axis=1).astype(jnp.int32)
    block_size = min(256, PCAP)
    block_count = NPROBE // block_size

    def one_block(start):
        rows_index = lax.dynamic_slice_in_dim(cell_index, start, block_size, 0)
        context = jnp.take(flat_ext, rows_index, axis=0)
        offsets = lax.dynamic_slice_in_dim(probe_offset, start, block_size, 1)
        return decode_block(context, offsets, w_query, w_head)
    starts = jnp.arange(block_count, dtype=jnp.int32) * block_size
    values = lax.map(one_block, starts).reshape(NPROBE, CH)
    live = slots % PCAP < probe_count[device]
    probe_values = jnp.where(live[None, :], values.T, jnp.zeros((), jnp.float32))
    return (latent, probe_values)
```

```python
import functools
import math

import jax
import jax.numpy as jnp
import numpy as np
from jax import lax
from jax.experimental import pallas as pl
from jax.experimental.pallas import tpu as pltpu
from jax.sharding import PartitionSpec as P

HEADS = 12
FQ = 128
CH = 3
RAD = 3
STEPS = 2
EPS = 1e-06
NOISE_COEF = 0.3
MESH = pl.DeviceIdType.MESH
FAR = -1e30
LANES = 128
SIDES = [(dr, dc) for dc in (-1, 1) for dr in (-1, 0, 1)]
F32 = jnp.float32
BF16 = jnp.bfloat16


def side_rows(rows, width):
    return -(-(rows + 2 * width) * width // 8) * 8


def side_cells(rows, cols, width):
    held = side_rows(rows, width)
    places = []
    for first in (-width, cols):
        group = [(r, first + c) for r in range(-width, rows + width) for c in range(width)]
        places += group + [None] * (held - len(group))
    return places


def halo_cells(rows, cols, width):
    own = [(r, c) for r in range(rows) for c in range(cols)]
    above = [(r, c) for r in range(-width, 0) for c in range(cols)]
    below = [(r, c) for r in range(rows, rows + width) for c in range(cols)]
    return own + above + below + side_cells(rows, cols, width)


def packet_table(rows, cols, width):
    places = side_cells(rows, cols, width)
    table = np.zeros((len(SIDES), len(places), rows * cols), np.float32)
    for number, (dr, dc) in enumerate(SIDES):
        for place, cell in enumerate(places):
            if cell is None:
                continue
            r, c = cell[0] + dr * rows, cell[1] + dc * cols
            if 0 <= r < rows and 0 <= c < cols:
                table[number, place, r * cols + c] = 1.0
    return table


def window_bias(rows, cols, width):
    cells = halo_cells(rows, cols, width)
    bias = np.full((len(cells), rows * cols), FAR, np.float32)
    for place, cell in enumerate(cells):
        if cell is None:
            continue
        for r in range(rows):
            for c in range(cols):
                if abs(cell[0] - r) <= width and abs(cell[1] - c) <= width:
                    bias[place, r * cols + c] = 0.0
    return bias


def sine_terms(t):
    z = (t * t) * (4.0 * math.pi * math.pi)
    odd = jnp.full_like(t, -1.0 / math.factorial(15))
    for power in range(13, 0, -2):
        odd = odd * z + (-1.0) ** (power // 2) / math.factorial(power)
    even = jnp.full_like(t, 1.0 / math.factorial(16))
    for power in range(14, -1, -2):
        even = even * z + (-1.0) ** (power // 2) / math.factorial(power)
    return odd * (t * (2.0 * math.pi)), even


def dot(a, b):
    return lax.dot_general(a, b, (((1,), (0,)), ((), ())), preferred_element_type=F32)


def dot_t(a, b):
    return lax.dot_general(a, b, (((1,), (1,)), ((), ())), preferred_element_type=F32)


def body(dims, gather, *refs):
    n_gx, n_gy, n_pa, rows, cols, model = dims
    (lat_ref, noise_ref, gain_ref, cell_ref, offset_ref, near_bias_ref, probe_bias_ref, near_pick_ref,
     probe_pick_ref, *refs) = refs
    weight_in, refs = refs[:4], refs[4:]
    out_ref, val_ref, *refs = refs
    if gather:
        weights, refs = refs[:4], refs[4:]
        w_send, w_recv, *refs = refs
    else:
        weights = weight_in
    (held0, held1, held2, got0, got1, got2, pack0, pack1, pack2, h_send, h_recv, normed, q_s, kv_s, att_s,
     hot_s, feat_s, qt_s, ut_s) = refs
    held, got, pack = (held0, held1, held2), (got0, got1, got2), (pack0, pack1, pack2)
    own = rows * cols
    gx, gy, pa = lax.axis_index("gx"), lax.axis_index("gy"), lax.axis_index("pa")
    ring = n_gx * n_pa
    place = gx * n_pa + pa

    def device(dr, dc):
        r = lax.rem(place + dr + ring, ring)
        return (lax.div(r, n_pa), lax.rem(gy + dc + n_gy, n_gy), lax.rem(r, n_pa))

    around = [device(-1, 0), device(1, 0)] + [device(dr, dc) for dr, dc in SIDES]
    partners = list(around)
    if gather:
        pa_x = lax.rem(pa + 2, 4)
        to_x, to_y = (gx, gy, pa_x), (1 - gx, gy, pa)
        to_twin = (gx, gy, pa + 1 - 2 * lax.rem(pa, 2))
        partners += [to_x, to_y, to_twin]
    barrier = pltpu.get_barrier_semaphore()
    for target in partners:
        pl.semaphore_signal(barrier, inc=1, device_id=target, device_id_type=MESH)
    pl.semaphore_wait(barrier, len(partners))

    started = []

    def push(src, dst, send, recv, target):
        copy = pltpu.make_async_remote_copy(
            src_ref=src, dst_ref=dst, send_sem=send, recv_sem=recv, device_id=target, device_id_type=MESH
        )
        copy.start()
        started.append(copy)
        return copy

    def widths(number):
        return RAD if number < STEPS else 1

    def halo_start(number, source):
        width = widths(number)
        span = width * cols
        here, sems = held[number], (h_send.at[number], h_recv.at[number])
        copies = [
            push(source.at[pl.ds(0, span)], here.at[pl.ds(own + span, span)], sems[0].at[0], sems[1].at[0], around[0]),
            push(source.at[pl.ds(own - span, span)], here.at[pl.ds(own, span)], sems[0].at[1], sems[1].at[1], around[1]),
        ]
        pick = (near_pick_ref if number < STEPS else probe_pick_ref)
        tail = pack[number].shape[1]
        value = source[...]
        for k in range(len(SIDES)):
            pack[number][k] = dot(pick[k], value).astype(BF16)
        for k in range(len(SIDES)):
            copies.append(
                push(pack[number].at[k], got[number].at[k], sems[0].at[2 + k], sems[1].at[2 + k], around[2 + k])
            )
        return copies

    def halo_end(number, copies):
        for copy in copies:
            copy.wait_recv()
        total = got[number][0].astype(F32)
        for k in range(1, len(SIDES)):
            total = total + got[number][k].astype(F32)
        tail = total.shape[0]
        base = own + 2 * widths(number) * cols
        held[number][pl.ds(base, tail)] = total.astype(BF16)

    class Moves:
        def __init__(self, number):
            self.number, self.ref = number, weights[number]
            half = self.ref.shape[1] // 2
            self.cut = half if half % 16 == 0 else None
            self.slot = {}

        def go(self, slot, part, target, lo=None, size=None):
            view = self.ref.at[part] if lo is None else self.ref.at[part, pl.ds(lo, size)]
            self.slot[slot] = push(view, view, w_send.at[self.number, slot], w_recv.at[self.number, slot], target)

        def begin(self):
            self.go(0, place, to_x)
            self.go(1, place, to_y)
            self.go(2, place, to_twin)

        def middle(self):
            near_x, near_y = gx * 4 + pa_x, (1 - gx) * 4 + pa
            self.slot[0].wait_recv()
            if self.cut is None:
                self.go(3, near_x, to_y)
            else:
                self.go(3, near_x, to_y, 0, self.cut)
            self.go(5, near_x, to_twin)
            self.slot[1].wait_recv()
            if self.cut is not None:
                self.go(4, near_y, to_x, self.cut, self.cut)
            self.go(6, near_y, to_twin)

        def end(self):
            across = (1 - gx) * 4 + pa_x
            self.slot[3].wait_recv()
            if self.cut is None:
                self.go(7, across, to_twin)
            else:
                self.go(7, across, to_twin, 0, self.cut)
                self.slot[4].wait_recv()
                self.go(8, across, to_twin, self.cut, self.cut)

        def finish(self):
            for slot in (2, 5, 6, 7, 8):
                if slot in self.slot:
                    self.slot[slot].wait_recv()

    if gather:
        moves = [Moves(number) for number in range(4)]
        weights[0][place] = weight_in[0][...]
        moves[0].begin()
        for number in (1, 2):
            weights[number][place] = weight_in[number][...]
        weights[3][place] = jnp.zeros(weights[3].shape[1:], BF16)
        weights[3][place, :, 0:CH] = weight_in[3][...]

    halo = halo_start(0, lat_ref)
    held[0][pl.ds(0, own)] = lat_ref[...]

    slots = cell_ref.shape[1]
    cells = lax.broadcasted_iota(jnp.int32, (own, slots), 0)
    hot_s[...] = jnp.where(cells == cell_ref[...], 1.0, 0.0).astype(BF16)
    quarter = FQ // 4
    freq = lax.broadcasted_iota(jnp.int32, (quarter, slots), 0).astype(F32) + 1.0
    for axis in range(2):
        turns = freq * offset_ref[pl.ds(axis, 1), :]
        sine, cosine = sine_terms(turns - jnp.floor(turns + 0.5))
        feat_s[pl.ds(2 * axis * quarter, quarter)] = sine.astype(BF16)
        feat_s[pl.ds((2 * axis + 1) * quarter, quarter)] = cosine.astype(BF16)

    def normalize(number):
        values = held[number][...].astype(F32)
        factor = lax.rsqrt(jnp.mean(values * values, axis=-1, keepdims=True) + EPS)
        normed[...] = (values * factor * gain_ref[...]).astype(BF16)

    def whole(number):
        ref = weights[number]
        return ref[...].reshape(-1, ref.shape[-1])

    def columns(number, start, size):
        ref = weights[number]
        if len(ref.shape) == 3:
            return ref[:, :, pl.ds(start, size)].reshape(model, size)
        return ref[:, pl.ds(start, size)]

    pairs = model // LANES
    keys = kv_s.shape[0]
    tile = 256
    scale = 1.0 / math.sqrt(model // HEADS)

    def project():
        def queries(i, carry):
            start = pl.multiple_of(i * tile, tile)
            q_s[:, pl.ds(start, tile)] = (dot(normed[pl.ds(0, own)], columns(0, start, tile)) * scale).astype(BF16)
            return carry

        def key_values(i, carry):
            start = pl.multiple_of(i * tile, tile)
            kv_s[:, pl.ds(start, tile)] = dot(normed[...], columns(0, model + start, tile)).astype(BF16)
            return carry

        lax.fori_loop(0, model // tile, queries, 0)
        lax.fori_loop(0, 2 * model // tile, key_values, 0)

    def attend():
        lane = lax.broadcasted_iota(jnp.int32, (own, LANES), 1)
        low = lane < LANES // 2
        unit = jnp.where(lane == lax.broadcasted_iota(jnp.int32, (own, LANES), 0), 1.0, 0.0).astype(BF16)
        zero = jnp.zeros((own, LANES), BF16)
        ones = jnp.ones((keys, LANES), BF16)

        def pair(i, carry):
            start = pl.multiple_of(i * LANES, LANES)
            query = q_s[:, pl.ds(start, LANES)]
            both = jnp.concatenate(
                [
                    jnp.concatenate([unit, jnp.where(low, query, zero)], axis=1),
                    jnp.concatenate([unit, jnp.where(low, zero, query)], axis=1),
                ],
                axis=0,
            )
            key = jnp.concatenate([near_bias_ref[...], kv_s[:, pl.ds(start, LANES)]], axis=1)
            scores = dot_t(both, key)
            top = jnp.max(scores, axis=1, keepdims=True)
            weight = jnp.exp(scores - top).astype(BF16)
            value = jnp.concatenate(
                [kv_s[:, pl.ds(pl.multiple_of(model + start, LANES), LANES)], ones], axis=1
            )
            mixed = dot(weight, value)
            mixed = mixed[:, :LANES] / mixed[:, LANES:]
            att_s[:, pl.ds(start, LANES)] = jnp.where(low, mixed[:own], mixed[own:]).astype(BF16)
            return carry

        lax.fori_loop(0, pairs, pair, 0, unroll=2)

    def update(step, target):
        for start in range(0, model, tile):
            cut = pl.ds(start, tile)
            moved = dot(att_s[...], columns(1, start, tile))
            target[pl.ds(0, own), cut] = (
                held[step][pl.ds(0, own), cut].astype(F32)
                + moved / STEPS
                + NOISE_COEF * noise_ref[step, :, cut].astype(F32)
            ).astype(BF16)

    if gather:
        moves[0].middle()
        for number in (1, 2, 3):
            moves[number].begin()
    halo_end(0, halo)
    normalize(0)
    if gather:
        moves[0].end()
        moves[0].finish()
    project()
    if gather:
        for number in (1, 2, 3):
            moves[number].middle()
    attend()
    if gather:
        for number in (1, 2, 3):
            moves[number].end()
        moves[1].finish()
    update(0, held[1])
    halo = halo_start(1, held[1].at[pl.ds(0, own)])
    if gather:
        moves[2].finish()
        moves[3].finish()
    turned = whole(2).astype(F32).T.astype(BF16)
    for start in range(0, slots, tile):
        qt_s[:, pl.ds(start, tile)] = (dot(turned, feat_s[:, pl.ds(start, tile)]) * scale).astype(BF16)
    halo_end(1, halo)
    normalize(1)
    project()
    attend()
    update(1, held[2])
    halo = halo_start(2, held[2].at[pl.ds(0, own)])
    out_ref[...] = held[2][pl.ds(0, own)]
    halo_end(2, halo)

    near = held[2].shape[0]
    head = weights[3]
    half = LANES // 2
    for i in range(pairs):
        context = held[2][:, pl.ds(i * LANES, LANES)]
        matrix = whole(3)[i * LANES : (i + 1) * LANES]
        row = lax.broadcasted_iota(jnp.int32, matrix.shape, 0)
        for side in range(2):
            kept = jnp.where((row < half) == (side == 0), matrix, jnp.zeros_like(matrix))
            turned = dot(context, kept).T[0:16]
            line = lax.broadcasted_iota(jnp.int32, turned.shape, 0)
            ut_s[2 * i + side] = jnp.where(line == CH, 1.0, turned).astype(BF16)

    val_ref[...] = jnp.zeros_like(val_ref)

    def decode(i, carry):
        start = pl.multiple_of(i * LANES, LANES)
        key = jnp.concatenate([probe_bias_ref[...], held[2][:, pl.ds(start, LANES)]], axis=1)
        for first in range(0, slots, tile):
            cut = pl.ds(first, tile)
            hot = hot_s[:, cut]
            blank = jnp.zeros((half, tile), BF16)
            total = val_ref[:, cut]
            for side in range(2):
                query = qt_s[pl.ds(pl.multiple_of(start + side * half, half), half), cut]
                parts = [hot, query, blank] if side == 0 else [hot, blank, query]
                scores = dot(key, jnp.concatenate(parts, axis=0))
                top = jnp.max(scores, axis=0, keepdims=True)
                weight = jnp.exp(scores - top).astype(BF16)
                mixed = dot(ut_s[2 * i + side], weight)
                total = total + mixed[0:8] / mixed[CH : CH + 1]
            val_ref[:, cut] = total
        return carry

    lax.fori_loop(0, pairs, decode, 0)
    for copy in started:
        copy.wait_send()


def local(sizes, latents, noise, proc_gain, w_qkv, w_out, w_query, w_head, probe_cell, probe_offset, probe_count):
    n_gx, n_gy, n_pa = sizes
    rows, cols, model = latents.shape
    own = rows * cols
    slots = probe_cell.shape[0]
    shards = [w_qkv, w_out, w_query, w_head]
    gather = n_gx == 2 and n_pa == 4 and all(shard.shape[0] % 16 == 0 for shard in shards)
    count = n_gx * n_pa
    if not gather:
        shards = [lax.all_gather(shard, ("gx", "pa"), axis=0, tiled=True) for shard in shards]
        shards[3] = jnp.pad(shards[3], ((0, 0), (0, LANES - CH)))
    near = len(halo_cells(rows, cols, RAD))
    close = len(halo_cells(rows, cols, 1))
    side_near, side_close = 2 * side_rows(rows, RAD), 2 * side_rows(rows, 1)
    tables = [
        jnp.asarray(table, BF16)
        for table in (
            window_bias(rows, cols, RAD),
            window_bias(rows, cols, 1),
            packet_table(rows, cols, RAD),
            packet_table(rows, cols, 1),
        )
    ]
    scratch = []
    if gather:
        scratch += [pltpu.VMEM((count,) + shard.shape, BF16) for shard in shards[:3]]
        scratch += [pltpu.VMEM((count, w_head.shape[0], LANES), BF16)]
        scratch += [pltpu.SemaphoreType.DMA((4, 9)), pltpu.SemaphoreType.DMA((4, 9))]
    scratch += [pltpu.VMEM((size, model), BF16) for size in (near, near, close)]
    for _ in range(2):
        scratch += [pltpu.VMEM((len(SIDES), size, model), BF16) for size in (side_near, side_near, side_close)]
    scratch += [pltpu.SemaphoreType.DMA((STEPS + 1, 8)), pltpu.SemaphoreType.DMA((STEPS + 1, 8))]
    scratch += [
        pltpu.VMEM((near, model), BF16),
        pltpu.VMEM((own, model), BF16),
        pltpu.VMEM((near, 2 * model), BF16),
        pltpu.VMEM((own, model), BF16),
        pltpu.VMEM((own, slots), BF16),
        pltpu.VMEM((FQ, slots), BF16),
        pltpu.VMEM((model, slots), BF16),
        pltpu.VMEM((HEADS, 16, close), BF16),
    ]
    operands = [
        latents.reshape(own, model),
        noise.reshape(STEPS, own, model),
        proc_gain.reshape(1, model),
        probe_cell.reshape(1, slots),
        probe_offset,
        *tables,
        *shards,
    ]
    latent_out, values = pl.pallas_call(
        functools.partial(body, (n_gx, n_gy, n_pa, rows, cols, model), gather),
        out_shape=(jax.ShapeDtypeStruct((own, model), BF16), jax.ShapeDtypeStruct((8, slots), F32)),
        in_specs=[pl.BlockSpec(memory_space=pltpu.VMEM)] * len(operands),
        out_specs=[pl.BlockSpec(memory_space=pltpu.VMEM)] * 2,
        scratch_shapes=scratch,
        compiler_params=pltpu.CompilerParams(
            collective_id=0, has_side_effects=True, vmem_limit_bytes=48 * 1024 * 1024
        ),
        cost_estimate=pl.CostEstimate(flops=6_000_000_000, bytes_accessed=4_000_000, transcendentals=4_000_000),
    )(*operands)
    live = jnp.arange(slots, dtype=jnp.int32) < probe_count[0]
    probe_values = jnp.where(live[None, :], values[:CH], jnp.zeros((), F32))
    return (latent_out.reshape(rows, cols, model), probe_values)


def solution(mesh):
    sizes = (mesh.shape["gx"], mesh.shape["gy"], mesh.shape["pa"])
    return jax.shard_map(
        functools.partial(local, sizes),
        mesh=mesh,
        in_specs=(
            P(("gx", "pa"), "gy", None),
            P(None, ("gx", "pa"), "gy", None),
            P(),
            P(("gx", "pa"), None),
            P(("gx", "pa"), None),
            P(("gx", "pa"), None),
            P(("gx", "pa"), None),
            P(("gx", "gy", "pa")),
            P(None, ("gx", "gy", "pa")),
            P(("gx", "gy", "pa")),
        ),
        out_specs=(P(("gx", "pa"), "gy", None), P(None, ("gx", "gy", "pa"))),
        check_vma=False,
    )
```

```python
import functools
import math

import jax
import jax.numpy as jnp
import numpy as np
from jax import lax
from jax.experimental import pallas as pl
from jax.experimental.pallas import tpu as pltpu
from jax.sharding import PartitionSpec as P

HEADS = 12
FQ = 128
CH = 3
RAD = 3
STEPS = 2
EPS = 1e-06
NOISE_COEF = 0.3
MESH = pl.DeviceIdType.MESH
FAR = -1e30
LANES = 128
PACKET = 16
VMEM_BYTES = 63 * 1024 * 1024
SIDES = [(dr, dc) for dc in (-1, 1) for dr in (-1, 0, 1)]
F32 = jnp.float32
BF16 = jnp.bfloat16


def side_rows(rows, width):
    return -(-(rows + 2 * width) * width // 8) * 8


def side_cells(rows, cols, width):
    held = side_rows(rows, width)
    places = []
    for first in (-width, cols):
        group = [(r, first + c) for r in range(-width, rows + width) for c in range(width)]
        places += group + [None] * (held - len(group))
    return places


def halo_cells(rows, cols, width):
    own = [(r, c) for r in range(rows) for c in range(cols)]
    above = [(r, c) for r in range(-width, 0) for c in range(cols)]
    below = [(r, c) for r in range(rows, rows + width) for c in range(cols)]
    return own + above + below + side_cells(rows, cols, width)


def packet_tables(rows, cols, width):
    places = side_cells(rows, cols, width)
    pick = np.zeros((len(SIDES) * PACKET, rows * cols), np.float32)
    put = np.zeros((len(places), len(SIDES) * PACKET), np.float32)
    for number, (dr, dc) in enumerate(SIDES):
        line = number * PACKET
        for place, cell in enumerate(places):
            if cell is None:
                continue
            r, c = cell[0] + dr * rows, cell[1] + dc * cols
            if 0 <= r < rows and 0 <= c < cols:
                pick[line, r * cols + c] = 1.0
                put[place, line] = 1.0
                line += 1
        assert line <= (number + 1) * PACKET
    return pick, put


def window_bias(rows, cols, width):
    cells = halo_cells(rows, cols, width)
    bias = np.full((len(cells), rows * cols), FAR, np.float32)
    for place, cell in enumerate(cells):
        if cell is None:
            continue
        for r in range(rows):
            for c in range(cols):
                if abs(cell[0] - r) <= width and abs(cell[1] - c) <= width:
                    bias[place, r * cols + c] = 0.0
    return bias


def sine_terms(t):
    z = (t * t) * (4.0 * math.pi * math.pi)
    odd = jnp.full_like(t, -1.0 / math.factorial(15))
    for power in range(13, 0, -2):
        odd = odd * z + (-1.0) ** (power // 2) / math.factorial(power)
    even = jnp.full_like(t, 1.0 / math.factorial(16))
    for power in range(14, -1, -2):
        even = even * z + (-1.0) ** (power // 2) / math.factorial(power)
    return odd * (t * (2.0 * math.pi)), even


def dot(a, b):
    return lax.dot_general(a, b, (((1,), (0,)), ((), ())), preferred_element_type=F32)


def dot_t(a, b):
    return lax.dot_general(a, b, (((1,), (1,)), ((), ())), preferred_element_type=F32)


def body(dims, gather, *refs):
    n_gx, n_gy, n_pa, rows, cols, model = dims
    loads, refs = refs[:11], refs[11:]
    weight_in, refs = refs[:4], refs[4:]
    out_ref, val_ref, *refs = refs
    staged, refs = refs[:11], refs[11:]
    (noise_ref, gain_ref, cell_ref, offset_ref, near_bias_ref, probe_bias_ref, near_pick_ref, near_put_ref,
     probe_pick_ref, probe_put_ref) = staged[1:]
    held0 = staged[0]
    if gather:
        weights, refs = refs[:6], refs[6:]
        head_s, w_send, w_recv, w_here, *refs = refs
    (held1, held2, got0, got1, got2, pack0, pack1, pack2, h_send, h_recv, l_sem, normed, q_s, kv_s, att_s,
     hot_s, feat_s, qt_s, ut_s) = refs
    held, got, pack = (held0, held1, held2), (got0, got1, got2), (pack0, pack1, pack2)
    own = rows * cols
    gx, gy, pa = lax.axis_index("gx"), lax.axis_index("gy"), lax.axis_index("pa")
    ring = n_gx * n_pa
    place = gx * n_pa + pa

    local_copies = []
    for number, source in enumerate(loads):
        target = held0.at[pl.ds(0, own)] if number == 0 else staged[number]
        local_copies.append(pltpu.make_async_copy(source, target, l_sem.at[number]))
        local_copies[-1].start()

    def device(dr, dc):
        r = lax.rem(place + dr + ring, ring)
        return (lax.div(r, n_pa), lax.rem(gy + dc + n_gy, n_gy), lax.rem(r, n_pa))

    around = [device(-1, 0), device(1, 0)] + [device(dr, dc) for dr, dc in SIDES]
    partners = list(around)
    if gather:
        pa_x = lax.rem(pa + 2, 4)
        to_x, to_y = (gx, gy, pa_x), (1 - gx, gy, pa)
        to_twin = (gx, gy, pa + 1 - 2 * lax.rem(pa, 2))
        partners += [to_x, to_y, to_twin]
    barrier = pltpu.get_barrier_semaphore()
    for target in partners:
        pl.semaphore_signal(barrier, inc=1, device_id=target, device_id_type=MESH)
    pl.semaphore_wait(barrier, len(partners))

    started = []

    def push(src, dst, send, recv, target):
        copy = pltpu.make_async_remote_copy(
            src_ref=src, dst_ref=dst, send_sem=send, recv_sem=recv, device_id=target, device_id_type=MESH
        )
        copy.start()
        started.append(copy)
        return copy

    def widths(number):
        return RAD if number < STEPS else 1

    def halo_start(number):
        width = widths(number)
        span = width * cols
        here, send, recv = held[number], h_send.at[number], h_recv.at[number]
        copies = [
            push(here.at[pl.ds(0, span)], here.at[pl.ds(own + span, span)], send.at[0], recv.at[0], around[0]),
            push(here.at[pl.ds(own - span, span)], here.at[pl.ds(own, span)], send.at[1], recv.at[1], around[1]),
        ]
        pick = near_pick_ref if number < STEPS else probe_pick_ref
        pack[number][...] = dot(pick[...], here[pl.ds(0, own)]).astype(BF16)
        for k in range(len(SIDES)):
            part = pl.ds(k * PACKET, PACKET)
            copies.append(
                push(pack[number].at[part], got[number].at[part], send.at[2 + k], recv.at[2 + k], around[2 + k])
            )
        return copies

    def halo_end(number, copies):
        for copy in copies:
            copy.wait_recv()
        put = near_put_ref if number < STEPS else probe_put_ref
        base = own + 2 * widths(number) * cols
        held[number][pl.ds(base, put.shape[0])] = dot(put[...], got[number][...]).astype(BF16)

    class Moves:
        def __init__(self, number, source):
            self.number, self.ref, self.source = number, weights[number], source
            half = self.ref.shape[1] // 2
            self.cut = half if half % 16 == 0 else None
            self.slot = {}

        def send(self, slot, src, dst, target):
            self.slot[slot] = push(src, dst, w_send.at[self.number, slot], w_recv.at[self.number, slot], target)

        def go(self, slot, part, target, lo=None, size=None):
            view = self.ref.at[part] if lo is None else self.ref.at[part, pl.ds(lo, size)]
            self.send(slot, view, view, target)

        def begin(self):
            here = self.ref.at[place]
            self.send(0, self.source, here, to_x)
            self.send(1, self.source, here, to_y)
            self.send(2, self.source, here, to_twin)

        def middle(self):
            near_x, near_y = gx * 4 + pa_x, (1 - gx) * 4 + pa
            self.slot[0].wait_recv()
            if self.cut is None:
                self.go(3, near_x, to_y)
            else:
                self.go(3, near_x, to_y, 0, self.cut)
            self.go(5, near_x, to_twin)
            self.slot[1].wait_recv()
            if self.cut is not None:
                self.go(4, near_y, to_x, self.cut, self.cut)
            self.go(6, near_y, to_twin)

        def end(self):
            across = (1 - gx) * 4 + pa_x
            self.slot[3].wait_recv()
            if self.cut is None:
                self.go(7, across, to_twin)
            else:
                self.go(7, across, to_twin, 0, self.cut)
                self.slot[4].wait_recv()
                self.go(8, across, to_twin, self.cut, self.cut)

        def finish(self):
            for slot in (2, 5, 6, 7, 8):
                if slot in self.slot:
                    self.slot[slot].wait_recv()

    tile = 256
    pairs = model // LANES
    keys = kv_s.shape[0]
    half = LANES // 2
    slots = cell_ref.shape[1]
    scale = math.log2(math.e) / math.sqrt(model // HEADS)

    if gather:
        sources = [weight_in[0].at[:, pl.ds(i * model, model)] for i in range(3)] + [weight_in[1], weight_in[2]]
        here_copies = [
            pltpu.make_async_copy(source, weights[i].at[place], w_here.at[i]) for i, source in enumerate(sources)
        ]
        here_copies.append(pltpu.make_async_copy(weight_in[3], head_s, w_here.at[5]))
        move_q, move_k, move_v, move_out, move_query = [Moves(i, source) for i, source in enumerate(sources)]
        move_head = Moves(5, weights[5].at[place])
        move_k.begin()
        move_q.begin()
        for copy in here_copies:
            copy.start()

    for copy in local_copies:
        copy.wait()
    halo = halo_start(0)

    cells = lax.broadcasted_iota(jnp.int32, (own, slots), 0)
    hot_s[...] = jnp.where(cells == cell_ref[...], 1.0, 0.0).astype(BF16)
    quarter = FQ // 4
    freq = lax.broadcasted_iota(jnp.int32, (quarter, slots), 0).astype(F32) + 1.0
    for axis in range(2):
        turns = freq * offset_ref[pl.ds(axis, 1), :]
        sine, cosine = sine_terms(turns - jnp.floor(turns + 0.5))
        feat_s[pl.ds(2 * axis * quarter, quarter)] = sine.astype(BF16)
        feat_s[pl.ds((2 * axis + 1) * quarter, quarter)] = cosine.astype(BF16)
    if gather:
        for copy in here_copies:
            copy.wait()
        weights[5][place] = jnp.zeros(weights[5].shape[1:], BF16)
        weights[5][place, 0:CH, 0 : model // ring] = head_s[...]

    def normalize(number, lo, count):
        part = pl.ds(lo, count)
        values = held[number][part].astype(F32)
        factor = lax.rsqrt(jnp.mean(values * values, axis=-1, keepdims=True) + EPS)
        normed[part] = (values * factor * gain_ref[...].reshape(1, model)).astype(BF16)

    def columns(piece, start, size):
        if gather:
            return weights[piece][:, :, pl.ds(start, size)].reshape(model, size)
        if piece < 3:
            return weight_in[0][:, pl.ds(piece * model + start, size)]
        return weight_in[piece - 2][:, pl.ds(start, size)]

    def project(piece, lo, count):
        def block(i, carry):
            start = pl.multiple_of(i * tile, tile)
            made = dot(normed[pl.ds(lo, count)], columns(piece, start, tile))
            if piece == 0:
                q_s[pl.ds(lo, count), pl.ds(start, tile)] = (made * scale).astype(BF16)
            else:
                kv_s[pl.ds(lo, count), pl.ds((piece - 1) * model + start, tile)] = made.astype(BF16)
            return carry

        lax.fori_loop(0, model // tile, block, 0)

    def attend():
        lane = lax.broadcasted_iota(jnp.int32, (own, LANES), 1)
        low = lane < half
        unit = jnp.where(lane == lax.broadcasted_iota(jnp.int32, (own, LANES), 0), 1.0, 0.0).astype(BF16)
        zero = jnp.zeros((own, LANES), BF16)
        ones = jnp.ones((keys, LANES), BF16)

        def pair(i, carry):
            start = pl.multiple_of(i * LANES, LANES)
            query = q_s[:, pl.ds(start, LANES)]
            both = jnp.concatenate(
                [
                    jnp.concatenate([unit, jnp.where(low, query, zero)], axis=1),
                    jnp.concatenate([unit, jnp.where(low, zero, query)], axis=1),
                ],
                axis=0,
            )
            key = jnp.concatenate([near_bias_ref[...], kv_s[:, pl.ds(start, LANES)]], axis=1)
            scores = dot_t(both, key)
            top = jnp.max(scores, axis=1, keepdims=True)
            weight = jnp.exp2(scores - top).astype(BF16)
            value = jnp.concatenate(
                [kv_s[:, pl.ds(pl.multiple_of(model + start, LANES), LANES)], ones], axis=1
            )
            mixed = dot(weight, value)
            mixed = mixed[:, :LANES] / mixed[:, LANES:]
            att_s[:, pl.ds(start, LANES)] = jnp.where(low, mixed[:own], mixed[own:]).astype(BF16)
            return carry

        lax.fori_loop(0, pairs, pair, 0, unroll=2)

    def update(step):
        for start in range(0, model, tile):
            cut = pl.ds(start, tile)
            moved = dot(att_s[...], columns(3, start, tile))
            held[step + 1][pl.ds(0, own), cut] = (
                held[step][pl.ds(0, own), cut].astype(F32)
                + moved / STEPS
                + NOISE_COEF * noise_ref[step, :, cut].astype(F32)
            ).astype(BF16)

    if gather:
        move_k.middle()
        move_v.begin()
    halo_end(0, halo)
    normalize(0, 0, keys)
    if gather:
        move_q.middle()
        move_out.begin()
        move_k.end()
        move_v.middle()
        move_query.begin()
        move_head.begin()
        move_q.end()
        move_k.finish()
    project(1, 0, keys)
    if gather:
        move_out.middle()
        move_v.end()
        move_q.finish()
    project(0, 0, own)
    if gather:
        move_query.middle()
        move_head.middle()
        move_out.end()
        move_v.finish()
    project(2, 0, keys)
    attend()
    if gather:
        move_query.end()
        move_head.end()
        move_out.finish()
    update(0)
    halo = halo_start(1)
    normalize(1, 0, own)
    for piece in range(3):
        project(piece, 0, own)
    if gather:
        move_query.finish()
        move_head.finish()
    turned = (
        weights[4][...].reshape(FQ, model) if gather else weight_in[2][...]
    )
    turned = turned.astype(F32).T.astype(BF16)
    for start in range(0, slots, tile):
        qt_s[:, pl.ds(start, tile)] = (dot(turned, feat_s[:, pl.ds(start, tile)]) * scale).astype(BF16)
    halo_end(1, halo)
    normalize(1, own, keys - own)
    project(1, own, keys - own)
    project(2, own, keys - own)
    attend()
    update(1)
    halo = halo_start(2)
    out_ref[...] = held2[pl.ds(0, own)]
    if gather:
        head = jnp.concatenate([weights[5][j, :, 0 : model // ring] for j in range(ring)], axis=1)
    else:
        head = weight_in[3][...]
    every = jnp.concatenate([head.astype(F32)] * HEADS, axis=0)
    line = lax.broadcasted_iota(jnp.int32, every.shape, 0) // 16
    owner = lax.broadcasted_iota(jnp.int32, every.shape, 1) // (model // HEADS)
    every = jnp.where(line == owner, every, 0.0).astype(BF16)
    val_ref[...] = jnp.zeros_like(val_ref)
    halo_end(2, halo)
    near = held2.shape[0]
    turned = dot_t(every, held2[...])
    line = lax.rem(lax.broadcasted_iota(jnp.int32, turned.shape, 0), 16)
    ut_s[...] = jnp.where(line == CH, 1.0, turned).astype(BF16).reshape(HEADS, 16, near)

    def decode(i, carry):
        start = pl.multiple_of(i * LANES, LANES)
        key = jnp.concatenate([probe_bias_ref[...], held2[:, pl.ds(start, LANES)]], axis=1)
        for first in range(0, slots, tile):
            cut = pl.ds(first, tile)
            hot = hot_s[:, cut]
            blank = jnp.zeros((half, tile), BF16)
            total = val_ref[:, cut]
            for side in range(2):
                query = qt_s[pl.ds(pl.multiple_of(start + side * half, half), half), cut]
                parts = [hot, query, blank] if side == 0 else [hot, blank, query]
                scores = dot(key, jnp.concatenate(parts, axis=0))
                top = jnp.max(scores, axis=0, keepdims=True)
                weight = jnp.exp2(scores - top).astype(BF16)
                mixed = dot(ut_s[2 * i + side], weight)
                total = total + mixed[0:8] / mixed[CH : CH + 1]
            val_ref[:, cut] = total
        return carry

    lax.fori_loop(0, pairs, decode, 0)
    for copy in started:
        copy.wait_send()


def local(sizes, latents, noise, proc_gain, w_qkv, w_out, w_query, w_head, probe_cell, probe_offset, probe_count):
    n_gx, n_gy, n_pa = sizes
    rows, cols, model = latents.shape
    own = rows * cols
    slots = probe_cell.shape[0]
    shards = [w_qkv, w_out, w_query, w_head]
    gather = n_gx == 2 and n_pa == 4 and all(shard.shape[0] % 16 == 0 for shard in shards)
    count = n_gx * n_pa
    if not gather:
        shards = [lax.all_gather(shard, ("gx", "pa"), axis=0, tiled=True) for shard in shards]
        shards[3] = jnp.pad(shards[3].T, ((0, 16 - CH), (0, 0)))
    else:
        shards[3] = w_head.T
    near = len(halo_cells(rows, cols, RAD))
    close = len(halo_cells(rows, cols, 1))
    tables = [
        jnp.asarray(table, BF16)
        for table in (
            window_bias(rows, cols, RAD),
            window_bias(rows, cols, 1),
            *packet_tables(rows, cols, RAD),
            *packet_tables(rows, cols, 1),
        )
    ]
    loads = [
        latents.reshape(own, model),
        noise.reshape(STEPS, own, model),
        proc_gain,
        probe_cell.reshape(1, slots),
        probe_offset,
        *tables,
    ]
    scratch = [pltpu.VMEM((near, model), BF16)] + [pltpu.VMEM(load.shape, load.dtype) for load in loads[1:]]
    if gather:
        block = (count, w_out.shape[0], model)
        scratch += [pltpu.VMEM(block, BF16)] * 4
        scratch += [pltpu.VMEM((count,) + w_query.shape, BF16), pltpu.VMEM((count, 16, LANES), BF16)]
        scratch += [pltpu.VMEM(shards[3].shape, BF16)]
        scratch += [pltpu.SemaphoreType.DMA((6, 9)), pltpu.SemaphoreType.DMA((6, 9)), pltpu.SemaphoreType.DMA((6,))]
    scratch += [pltpu.VMEM((size, model), BF16) for size in (near, close)]
    scratch += [pltpu.VMEM((len(SIDES) * PACKET, model), BF16)] * 6
    scratch += [pltpu.SemaphoreType.DMA((STEPS + 1, 8)), pltpu.SemaphoreType.DMA((STEPS + 1, 8))]
    scratch += [pltpu.SemaphoreType.DMA((len(loads),))]
    scratch += [
        pltpu.VMEM((near, model), BF16),
        pltpu.VMEM((own, model), BF16),
        pltpu.VMEM((near, 2 * model), BF16),
        pltpu.VMEM((own, model), BF16),
        pltpu.VMEM((own, slots), BF16),
        pltpu.VMEM((FQ, slots), BF16),
        pltpu.VMEM((model, slots), BF16),
        pltpu.VMEM((HEADS, 16, close), BF16),
    ]
    apart = pl.BlockSpec(memory_space=pltpu.HBM)
    inside = pl.BlockSpec(memory_space=pltpu.VMEM)
    latent_out, values = pl.pallas_call(
        functools.partial(body, (n_gx, n_gy, n_pa, rows, cols, model), gather),
        out_shape=(jax.ShapeDtypeStruct((own, model), BF16), jax.ShapeDtypeStruct((8, slots), F32)),
        in_specs=[apart] * len(loads) + [apart if gather else inside] * len(shards),
        out_specs=[inside] * 2,
        scratch_shapes=scratch,
        compiler_params=pltpu.CompilerParams(
            collective_id=0, has_side_effects=True, vmem_limit_bytes=VMEM_BYTES
        ),
        cost_estimate=pl.CostEstimate(flops=6_000_000_000, bytes_accessed=4_000_000, transcendentals=4_000_000),
    )(*loads, *shards)
    live = jnp.arange(slots, dtype=jnp.int32) < probe_count[0]
    probe_values = jnp.where(live[None, :], values[:CH], jnp.zeros((), F32))
    return (latent_out.reshape(rows, cols, model), probe_values)


def solution(mesh):
    sizes = (mesh.shape["gx"], mesh.shape["gy"], mesh.shape["pa"])
    return jax.shard_map(
        functools.partial(local, sizes),
        mesh=mesh,
        in_specs=(
            P(("gx", "pa"), "gy", None),
            P(None, ("gx", "pa"), "gy", None),
            P(),
            P(("gx", "pa"), None),
            P(("gx", "pa"), None),
            P(("gx", "pa"), None),
            P(("gx", "pa"), None),
            P(("gx", "gy", "pa")),
            P(None, ("gx", "gy", "pa")),
            P(("gx", "gy", "pa")),
        ),
        out_specs=(P(("gx", "pa"), "gy", None), P(None, ("gx", "gy", "pa"))),
        check_vma=False,
    )
```

```python
import functools
import math

import jax
import jax.numpy as jnp
import numpy as np
from jax import lax
from jax.experimental import pallas as pl
from jax.experimental.pallas import tpu as pltpu
from jax.sharding import PartitionSpec as P

HEADS = 12
FQ = 128
CH = 3
RAD = 3
STEPS = 2
EPS = 1e-06
NOISE_COEF = 0.3
MESH = pl.DeviceIdType.MESH
FAR = -1e30
LANES = 128
PACKET = 16
VMEM_BYTES = 61 * 1024 * 1024
SIDES = [(dr, dc) for dc in (-1, 1) for dr in (-1, 0, 1)]
F32 = jnp.float32
BF16 = jnp.bfloat16


def side_rows(rows, width):
    return -(-(rows + 2 * width) * width // 8) * 8


def side_cells(rows, cols, width):
    held = side_rows(rows, width)
    places = []
    for first in (-width, cols):
        group = [(r, first + c) for r in range(-width, rows + width) for c in range(width)]
        places += group + [None] * (held - len(group))
    return places


def halo_cells(rows, cols, width):
    own = [(r, c) for r in range(rows) for c in range(cols)]
    above = [(r, c) for r in range(-width, 0) for c in range(cols)]
    below = [(r, c) for r in range(rows, rows + width) for c in range(cols)]
    return own + above + below + side_cells(rows, cols, width)


def packet_tables(rows, cols, width):
    places = side_cells(rows, cols, width)
    pick = np.zeros((len(SIDES) * PACKET, rows * cols), np.float32)
    put = np.zeros((len(places), len(SIDES) * PACKET), np.float32)
    for number, (dr, dc) in enumerate(SIDES):
        line = number * PACKET
        for place, cell in enumerate(places):
            if cell is None:
                continue
            r, c = cell[0] + dr * rows, cell[1] + dc * cols
            if 0 <= r < rows and 0 <= c < cols:
                pick[line, r * cols + c] = 1.0
                put[place, line] = 1.0
                line += 1
        assert line <= (number + 1) * PACKET
    return pick, put


def window_bias(rows, cols, width):
    cells = halo_cells(rows, cols, width)
    bias = np.full((len(cells), rows * cols), FAR, np.float32)
    for place, cell in enumerate(cells):
        if cell is None:
            continue
        for r in range(rows):
            for c in range(cols):
                if abs(cell[0] - r) <= width and abs(cell[1] - c) <= width:
                    bias[place, r * cols + c] = 0.0
    return bias


def sine_terms(t):
    z = (t * t) * (4.0 * math.pi * math.pi)
    odd = jnp.full_like(t, -1.0 / math.factorial(15))
    for power in range(13, 0, -2):
        odd = odd * z + (-1.0) ** (power // 2) / math.factorial(power)
    even = jnp.full_like(t, 1.0 / math.factorial(16))
    for power in range(14, -1, -2):
        even = even * z + (-1.0) ** (power // 2) / math.factorial(power)
    return odd * (t * (2.0 * math.pi)), even


def dot(a, b):
    return lax.dot_general(a, b, (((1,), (0,)), ((), ())), preferred_element_type=F32)


def dot_t(a, b):
    return lax.dot_general(a, b, (((1,), (1,)), ((), ())), preferred_element_type=F32)


def body(dims, gather, *refs):
    n_gx, n_gy, n_pa, rows, cols, model = dims
    loads, refs = refs[:11], refs[11:]
    weight_in, refs = refs[:4], refs[4:]
    out_ref, val_ref, *refs = refs
    staged, refs = refs[:11], refs[11:]
    (noise_ref, gain_ref, cell_ref, offset_ref, near_bias_ref, probe_bias_ref, near_pick_ref, near_put_ref,
     probe_pick_ref, probe_put_ref) = staged[1:]
    held0 = staged[0]
    if gather:
        weights, refs = refs[:6], refs[6:]
        head_s, w_send, w_recv, w_here, *refs = refs
    (held1, held2, got0, got1, got2, pack0, pack1, pack2, h_send, h_recv, l_sem, normed, q_s, kv_s, att_s,
     hot_s, feat_s, qt_s, ut_s) = refs
    held, got, pack = (held0, held1, held2), (got0, got1, got2), (pack0, pack1, pack2)
    own = rows * cols
    gx, gy, pa = lax.axis_index("gx"), lax.axis_index("gy"), lax.axis_index("pa")
    ring = n_gx * n_pa
    place = gx * n_pa + pa

    local_copies = []
    for number, source in enumerate(loads):
        target = held0.at[pl.ds(0, own)] if number == 0 else staged[number]
        local_copies.append(pltpu.make_async_copy(source, target, l_sem.at[number]))
        local_copies[-1].start()

    def device(dr, dc):
        r = lax.rem(place + dr + ring, ring)
        return (lax.div(r, n_pa), lax.rem(gy + dc + n_gy, n_gy), lax.rem(r, n_pa))

    around = [device(-1, 0), device(1, 0)] + [device(dr, dc) for dr, dc in SIDES]
    partners = list(around)
    if gather:
        pa_x = lax.rem(pa + 2, 4)
        to_x, to_y = (gx, gy, pa_x), (1 - gx, gy, pa)
        to_twin = (gx, gy, pa + 1 - 2 * lax.rem(pa, 2))
        partners += [to_x, to_y, to_twin]
    barrier = pltpu.get_barrier_semaphore()
    for target in partners:
        pl.semaphore_signal(barrier, inc=1, device_id=target, device_id_type=MESH)
    pl.semaphore_wait(barrier, len(partners))

    started = []

    def push(src, dst, send, recv, target):
        copy = pltpu.make_async_remote_copy(
            src_ref=src, dst_ref=dst, send_sem=send, recv_sem=recv, device_id=target, device_id_type=MESH
        )
        copy.start()
        started.append(copy)
        return copy

    def widths(number):
        return RAD if number < STEPS else 1

    def halo_start(number):
        width = widths(number)
        span = width * cols
        here, send, recv = held[number], h_send.at[number], h_recv.at[number]
        copies = [
            push(here.at[pl.ds(0, span)], here.at[pl.ds(own + span, span)], send.at[0], recv.at[0], around[0]),
            push(here.at[pl.ds(own - span, span)], here.at[pl.ds(own, span)], send.at[1], recv.at[1], around[1]),
        ]
        pick = near_pick_ref if number < STEPS else probe_pick_ref
        pack[number][...] = dot(pick[...], here[pl.ds(0, own)]).astype(BF16)
        for k in range(len(SIDES)):
            part = pl.ds(k * PACKET, PACKET)
            copies.append(
                push(pack[number].at[part], got[number].at[part], send.at[2 + k], recv.at[2 + k], around[2 + k])
            )
        return copies

    def halo_end(number, copies):
        for copy in copies:
            copy.wait_recv()
        put = near_put_ref if number < STEPS else probe_put_ref
        base = own + 2 * widths(number) * cols
        held[number][pl.ds(base, put.shape[0])] = dot(put[...], got[number][...]).astype(BF16)

    class Moves:
        def __init__(self, number, source):
            self.number, self.ref, self.source = number, weights[number], source
            half = self.ref.shape[1] // 2
            self.cut = half if half % 16 == 0 else None
            self.slot = {}

        def send(self, slot, src, dst, target):
            self.slot[slot] = push(src, dst, w_send.at[self.number, slot], w_recv.at[self.number, slot], target)

        def go(self, slot, part, target, lo=None, size=None):
            view = self.ref.at[part] if lo is None else self.ref.at[part, pl.ds(lo, size)]
            self.send(slot, view, view, target)

        def begin(self):
            here = self.ref.at[place]
            self.send(0, self.source, here, to_x)
            self.send(1, self.source, here, to_y)
            self.send(2, self.source, here, to_twin)

        def middle(self):
            near_x, near_y = gx * 4 + pa_x, (1 - gx) * 4 + pa
            self.slot[0].wait_recv()
            if self.cut is None:
                self.go(3, near_x, to_y)
            else:
                self.go(3, near_x, to_y, 0, self.cut)
            self.go(5, near_x, to_twin)
            self.slot[1].wait_recv()
            if self.cut is not None:
                self.go(4, near_y, to_x, self.cut, self.cut)
            self.go(6, near_y, to_twin)

        def end(self):
            across = (1 - gx) * 4 + pa_x
            self.slot[3].wait_recv()
            if self.cut is None:
                self.go(7, across, to_twin)
            else:
                self.go(7, across, to_twin, 0, self.cut)
                self.slot[4].wait_recv()
                self.go(8, across, to_twin, self.cut, self.cut)

        def finish(self):
            for slot in (2, 5, 6, 7, 8):
                if slot in self.slot:
                    self.slot[slot].wait_recv()

    tile = 256
    pairs = model // LANES
    keys = kv_s.shape[0]
    half = LANES // 2
    slots = cell_ref.shape[1]
    scale = math.log2(math.e) / math.sqrt(model // HEADS)

    if gather:
        sources = [weight_in[0].at[:, pl.ds(i * model, model)] for i in range(3)] + [weight_in[1], weight_in[2]]
        here_copies = [
            pltpu.make_async_copy(source, weights[i].at[place], w_here.at[i]) for i, source in enumerate(sources)
        ]
        here_copies.append(pltpu.make_async_copy(weight_in[3], head_s, w_here.at[5]))
        move_q, move_k, move_v, move_out, move_query = [Moves(i, source) for i, source in enumerate(sources)]
        move_head = Moves(5, weights[5].at[place])
        for copy in here_copies[::-1]:
            copy.start()
        move_query.begin()
        move_k.begin()
        move_q.begin()
        here_copies[5].wait()
        weights[5][place] = jnp.zeros(weights[5].shape[1:], BF16)
        weights[5][place, 0:CH, 0 : model // ring] = head_s[...]
        move_head.begin()

    for copy in local_copies:
        copy.wait()
    halo = halo_start(0)

    cells = lax.broadcasted_iota(jnp.int32, (own, slots), 0)
    hot_s[...] = jnp.where(cells == cell_ref[...], 1.0, 0.0).astype(BF16)
    quarter = FQ // 4
    freq = lax.broadcasted_iota(jnp.int32, (quarter, slots), 0).astype(F32) + 1.0
    for axis in range(2):
        turns = freq * offset_ref[pl.ds(axis, 1), :]
        sine, cosine = sine_terms(turns - jnp.floor(turns + 0.5))
        feat_s[pl.ds(2 * axis * quarter, quarter)] = sine.astype(BF16)
        feat_s[pl.ds((2 * axis + 1) * quarter, quarter)] = cosine.astype(BF16)
    if gather:
        move_query.middle()
        move_head.middle()
        for copy in here_copies[:5]:
            copy.wait()

    def normalize(number, lo, count):
        part = pl.ds(lo, count)
        values = held[number][part].astype(F32)
        factor = lax.rsqrt(jnp.mean(values * values, axis=-1, keepdims=True) + EPS)
        normed[part] = (values * factor * gain_ref[...].reshape(1, model)).astype(BF16)

    def columns(piece, start, size):
        if gather:
            return weights[piece][:, :, pl.ds(start, size)].reshape(model, size)
        if piece < 3:
            return weight_in[0][:, pl.ds(piece * model + start, size)]
        return weight_in[piece - 2][:, pl.ds(start, size)]

    def project(piece, lo, count):
        def block(i, carry):
            start = pl.multiple_of(i * tile, tile)
            made = dot(normed[pl.ds(lo, count)], columns(piece, start, tile))
            if piece == 0:
                q_s[pl.ds(lo, count), pl.ds(start, tile)] = (made * scale).astype(BF16)
            else:
                kv_s[pl.ds(lo, count), pl.ds((piece - 1) * model + start, tile)] = made.astype(BF16)
            return carry

        lax.fori_loop(0, model // tile, block, 0, unroll=True)

    def attend():
        lane = lax.broadcasted_iota(jnp.int32, (own, LANES), 1)
        low = lane < half
        unit = jnp.where(lane == lax.broadcasted_iota(jnp.int32, (own, LANES), 0), 1.0, 0.0).astype(BF16)
        zero = jnp.zeros((own, LANES), BF16)
        ones = jnp.ones((keys, LANES), BF16)

        def pair(i, carry):
            start = pl.multiple_of(i * LANES, LANES)
            query = q_s[:, pl.ds(start, LANES)]
            both = jnp.concatenate(
                [
                    jnp.concatenate([unit, jnp.where(low, query, zero)], axis=1),
                    jnp.concatenate([unit, jnp.where(low, zero, query)], axis=1),
                ],
                axis=0,
            )
            key = jnp.concatenate([near_bias_ref[...], kv_s[:, pl.ds(start, LANES)]], axis=1)
            scores = dot_t(both, key)
            top = jnp.max(scores, axis=1, keepdims=True)
            weight = jnp.exp2(scores - top).astype(BF16)
            value = jnp.concatenate(
                [kv_s[:, pl.ds(pl.multiple_of(model + start, LANES), LANES)], ones], axis=1
            )
            mixed = dot(weight, value)
            mixed = mixed[:, :LANES] / mixed[:, LANES:]
            att_s[:, pl.ds(start, LANES)] = jnp.where(low, mixed[:own], mixed[own:]).astype(BF16)
            return carry

        lax.fori_loop(0, pairs, pair, 0, unroll=3 if pairs % 3 == 0 else 1)

    def update(step):
        for start in range(0, model, tile):
            cut = pl.ds(start, tile)
            moved = dot(att_s[...], columns(3, start, tile))
            held[step + 1][pl.ds(0, own), cut] = (
                held[step][pl.ds(0, own), cut].astype(F32)
                + moved / STEPS
                + NOISE_COEF * noise_ref[step, :, cut].astype(F32)
            ).astype(BF16)

    halo_end(0, halo)
    normalize(0, 0, keys)
    if gather:
        move_query.end()
        move_head.end()
        move_k.middle()
        move_v.begin()
        move_query.finish()
        move_head.finish()
    turned = weights[4][...].reshape(FQ, model) if gather else weight_in[2][...]
    turned = turned.astype(F32).T.astype(BF16)
    for start in range(0, slots, tile):
        qt_s[:, pl.ds(start, tile)] = (dot(turned, feat_s[:, pl.ds(start, tile)]) * scale).astype(BF16)
    if gather:
        move_q.middle()
        move_k.end()
        move_v.middle()
        move_out.begin()
        move_q.end()
        move_k.finish()
    project(1, 0, keys)
    if gather:
        move_q.finish()
    project(0, 0, own)
    if gather:
        move_v.end()
        move_out.middle()
        move_v.finish()
    project(2, 0, keys)
    attend()
    if gather:
        move_out.end()
        move_out.finish()
    update(0)
    halo = halo_start(1)
    normalize(1, 0, own)
    for piece in range(3):
        project(piece, 0, own)
    halo_end(1, halo)
    normalize(1, own, keys - own)
    project(1, own, keys - own)
    project(2, own, keys - own)
    attend()
    update(1)
    halo = halo_start(2)
    out_ref[...] = held2[pl.ds(0, own)]
    if gather:
        head = jnp.concatenate([weights[5][j, :, 0 : model // ring] for j in range(ring)], axis=1)
    else:
        head = weight_in[3][...]
    every = jnp.concatenate([head.astype(F32)] * HEADS, axis=0)
    line = lax.broadcasted_iota(jnp.int32, every.shape, 0) // 16
    owner = lax.broadcasted_iota(jnp.int32, every.shape, 1) // (model // HEADS)
    every = jnp.where(line == owner, every, 0.0).astype(BF16)
    val_ref[...] = jnp.zeros_like(val_ref)
    halo_end(2, halo)
    near = held2.shape[0]
    turned = dot_t(every, held2[...])
    line = lax.rem(lax.broadcasted_iota(jnp.int32, turned.shape, 0), 16)
    ut_s[...] = jnp.where(line == CH, 1.0, turned).astype(BF16).reshape(HEADS, 16, near)

    def decode(i, carry):
        start = pl.multiple_of(i * LANES, LANES)
        context = held2[:, pl.ds(start, LANES)]
        low = lax.broadcasted_iota(jnp.int32, context.shape, 1) < half
        blank = jnp.zeros_like(context)
        key = jnp.concatenate(
            [
                jnp.concatenate([probe_bias_ref[...], jnp.where(low, context, blank)], axis=1),
                jnp.concatenate([probe_bias_ref[...], jnp.where(low, blank, context)], axis=1),
            ],
            axis=0,
        )
        for first in range(0, slots, tile):
            cut = pl.ds(first, tile)
            scores = dot(key, jnp.concatenate([hot_s[:, cut], qt_s[pl.ds(start, LANES), cut]], axis=0))
            total = val_ref[:, cut]
            for side in range(2):
                part = scores[side * near : (side + 1) * near]
                top = jnp.max(part, axis=0, keepdims=True)
                weight = jnp.exp2(part - top).astype(BF16)
                mixed = dot(ut_s[2 * i + side], weight)
                total = total + mixed[0:8] / mixed[CH : CH + 1]
            val_ref[:, cut] = total
        return carry

    lax.fori_loop(0, pairs, decode, 0)
    for copy in started:
        copy.wait_send()


def local(sizes, latents, noise, proc_gain, w_qkv, w_out, w_query, w_head, probe_cell, probe_offset, probe_count):
    n_gx, n_gy, n_pa = sizes
    rows, cols, model = latents.shape
    own = rows * cols
    slots = probe_cell.shape[0]
    shards = [w_qkv, w_out, w_query, w_head]
    gather = n_gx == 2 and n_pa == 4 and all(shard.shape[0] % 16 == 0 for shard in shards)
    count = n_gx * n_pa
    if not gather:
        shards = [lax.all_gather(shard, ("gx", "pa"), axis=0, tiled=True) for shard in shards]
        shards[3] = jnp.pad(shards[3].T, ((0, 16 - CH), (0, 0)))
    else:
        shards[3] = w_head.T
    near = len(halo_cells(rows, cols, RAD))
    close = len(halo_cells(rows, cols, 1))
    tables = [
        jnp.asarray(table, BF16)
        for table in (
            window_bias(rows, cols, RAD),
            window_bias(rows, cols, 1),
            *packet_tables(rows, cols, RAD),
            *packet_tables(rows, cols, 1),
        )
    ]
    loads = [
        latents.reshape(own, model),
        noise.reshape(STEPS, own, model),
        proc_gain,
        probe_cell.reshape(1, slots),
        probe_offset,
        *tables,
    ]
    scratch = [pltpu.VMEM((near, model), BF16)] + [pltpu.VMEM(load.shape, load.dtype) for load in loads[1:]]
    if gather:
        block = (count, w_out.shape[0], model)
        scratch += [pltpu.VMEM(block, BF16)] * 4
        scratch += [pltpu.VMEM((count,) + w_query.shape, BF16), pltpu.VMEM((count, 16, LANES), BF16)]
        scratch += [pltpu.VMEM(shards[3].shape, BF16)]
        scratch += [pltpu.SemaphoreType.DMA((6, 9)), pltpu.SemaphoreType.DMA((6, 9)), pltpu.SemaphoreType.DMA((6,))]
    scratch += [pltpu.VMEM((size, model), BF16) for size in (near, close)]
    scratch += [pltpu.VMEM((len(SIDES) * PACKET, model), BF16)] * 6
    scratch += [pltpu.SemaphoreType.DMA((STEPS + 1, 8)), pltpu.SemaphoreType.DMA((STEPS + 1, 8))]
    scratch += [pltpu.SemaphoreType.DMA((len(loads),))]
    scratch += [
        pltpu.VMEM((near, model), BF16),
        pltpu.VMEM((own, model), BF16),
        pltpu.VMEM((near, 2 * model), BF16),
        pltpu.VMEM((own, model), BF16),
        pltpu.VMEM((own, slots), BF16),
        pltpu.VMEM((FQ, slots), BF16),
        pltpu.VMEM((model, slots), BF16),
        pltpu.VMEM((HEADS, 16, close), BF16),
    ]
    apart = pl.BlockSpec(memory_space=pltpu.HBM)
    inside = pl.BlockSpec(memory_space=pltpu.VMEM)
    latent_out, values = pl.pallas_call(
        functools.partial(body, (n_gx, n_gy, n_pa, rows, cols, model), gather),
        out_shape=(jax.ShapeDtypeStruct((own, model), BF16), jax.ShapeDtypeStruct((8, slots), F32)),
        in_specs=[apart] * len(loads) + [apart if gather else inside] * len(shards),
        out_specs=[inside] * 2,
        scratch_shapes=scratch,
        compiler_params=pltpu.CompilerParams(
            collective_id=0, has_side_effects=True, vmem_limit_bytes=VMEM_BYTES
        ),
        cost_estimate=pl.CostEstimate(flops=6_000_000_000, bytes_accessed=4_000_000, transcendentals=4_000_000),
    )(*loads, *shards)
    live = jnp.arange(slots, dtype=jnp.int32) < probe_count[0]
    probe_values = jnp.where(live[None, :], values[:CH], jnp.zeros((), F32))
    return (latent_out.reshape(rows, cols, model), probe_values)


def solution(mesh):
    sizes = (mesh.shape["gx"], mesh.shape["gy"], mesh.shape["pa"])
    return jax.shard_map(
        functools.partial(local, sizes),
        mesh=mesh,
        in_specs=(
            P(("gx", "pa"), "gy", None),
            P(None, ("gx", "pa"), "gy", None),
            P(),
            P(("gx", "pa"), None),
            P(("gx", "pa"), None),
            P(("gx", "pa"), None),
            P(("gx", "pa"), None),
            P(("gx", "gy", "pa")),
            P(None, ("gx", "gy", "pa")),
            P(("gx", "gy", "pa")),
        ),
        out_specs=(P(("gx", "pa"), "gy", None), P(None, ("gx", "gy", "pa"))),
        check_vma=False,
    )
```

```python
import functools
import math

import jax
import jax.numpy as jnp
import numpy as np
from jax import lax
from jax.experimental import pallas as pl
from jax.experimental.pallas import tpu as pltpu
from jax.sharding import PartitionSpec as P

HEADS = 12
FQ = 128
CH = 3
RAD = 3
STEPS = 2
EPS = 1e-06
NOISE_COEF = 0.3
MESH = pl.DeviceIdType.MESH
FAR = -1e30
LANES = 128
PACKET = 16
VMEM_BYTES = 61 * 1024 * 1024
SIDES = [(dr, dc) for dc in (-1, 1) for dr in (-1, 0, 1)]
F32 = jnp.float32
BF16 = jnp.bfloat16


def side_rows(rows, width):
    return -(-(rows + 2 * width) * width // 8) * 8


def side_cells(rows, cols, width):
    held = side_rows(rows, width)
    places = []
    for first in (-width, cols):
        group = [(r, first + c) for r in range(-width, rows + width) for c in range(width)]
        places += group + [None] * (held - len(group))
    return places


def halo_cells(rows, cols, width):
    own = [(r, c) for r in range(rows) for c in range(cols)]
    above = [(r, c) for r in range(-width, 0) for c in range(cols)]
    below = [(r, c) for r in range(rows, rows + width) for c in range(cols)]
    return own + above + below + side_cells(rows, cols, width)


def packet_tables(rows, cols, width):
    places = side_cells(rows, cols, width)
    pick = np.zeros((len(SIDES) * PACKET, rows * cols), np.float32)
    put = np.zeros((len(places), len(SIDES) * PACKET), np.float32)
    for number, (dr, dc) in enumerate(SIDES):
        line = number * PACKET
        for place, cell in enumerate(places):
            if cell is None:
                continue
            r, c = cell[0] + dr * rows, cell[1] + dc * cols
            if 0 <= r < rows and 0 <= c < cols:
                pick[line, r * cols + c] = 1.0
                put[place, line] = 1.0
                line += 1
        assert line <= (number + 1) * PACKET
    return pick, put


def window_bias(rows, cols, width):
    cells = halo_cells(rows, cols, width)
    bias = np.full((len(cells), rows * cols), FAR, np.float32)
    for place, cell in enumerate(cells):
        if cell is None:
            continue
        for r in range(rows):
            for c in range(cols):
                if abs(cell[0] - r) <= width and abs(cell[1] - c) <= width:
                    bias[place, r * cols + c] = 0.0
    return bias


def sine_terms(t):
    z = (t * t) * (4.0 * math.pi * math.pi)
    odd = jnp.full_like(t, -1.0 / math.factorial(15))
    for power in range(13, 0, -2):
        odd = odd * z + (-1.0) ** (power // 2) / math.factorial(power)
    even = jnp.full_like(t, 1.0 / math.factorial(16))
    for power in range(14, -1, -2):
        even = even * z + (-1.0) ** (power // 2) / math.factorial(power)
    return odd * (t * (2.0 * math.pi)), even


def dot(a, b):
    return lax.dot_general(a, b, (((1,), (0,)), ((), ())), preferred_element_type=F32)


def dot_t(a, b):
    return lax.dot_general(a, b, (((1,), (1,)), ((), ())), preferred_element_type=F32)


def body(dims, gather, *refs):
    n_gx, n_gy, n_pa, rows, cols, model = dims
    loads, refs = refs[:11], refs[11:]
    weight_in, refs = refs[:4], refs[4:]
    out_ref, val_ref, *refs = refs
    staged, refs = refs[:11], refs[11:]
    (noise_ref, gain_ref, cell_ref, offset_ref, near_bias_ref, probe_bias_ref, near_pick_ref, near_put_ref,
     probe_pick_ref, probe_put_ref) = staged[1:]
    held0 = staged[0]
    if gather:
        weights, refs = refs[:6], refs[6:]
        head_s, w_send, w_recv, w_here, *refs = refs
    (held1, held2, got0, got1, got2, pack0, pack1, pack2, h_send, h_recv, l_sem, normed, q_s, kv_s, att_s,
     hot_s, feat_s, qt_s, ut_s, part_s, out_sem) = refs
    held, got, pack = (held0, held1, held2), (got0, got1, got2), (pack0, pack1, pack2)
    own = rows * cols
    gx, gy, pa = lax.axis_index("gx"), lax.axis_index("gy"), lax.axis_index("pa")
    ring = n_gx * n_pa
    place = gx * n_pa + pa

    local_copies = []
    for number, source in enumerate(loads):
        target = held0.at[pl.ds(0, own)] if number == 0 else staged[number]
        local_copies.append(pltpu.make_async_copy(source, target, l_sem.at[number]))
        local_copies[-1].start()

    def device(dr, dc):
        r = lax.rem(place + dr + ring, ring)
        return (lax.div(r, n_pa), lax.rem(gy + dc + n_gy, n_gy), lax.rem(r, n_pa))

    around = [device(-1, 0), device(1, 0)] + [device(dr, dc) for dr, dc in SIDES]
    partners = list(around)
    if gather:
        pa_x = lax.rem(pa + 2, 4)
        to_x, to_y = (gx, gy, pa_x), (1 - gx, gy, pa)
        to_twin = (gx, gy, pa + 1 - 2 * lax.rem(pa, 2))
        partners += [to_x, to_y, to_twin]
    barrier = pltpu.get_barrier_semaphore()
    for target in partners:
        pl.semaphore_signal(barrier, inc=1, device_id=target, device_id_type=MESH)
    pl.semaphore_wait(barrier, len(partners))

    started = []

    def push(src, dst, send, recv, target):
        copy = pltpu.make_async_remote_copy(
            src_ref=src, dst_ref=dst, send_sem=send, recv_sem=recv, device_id=target, device_id_type=MESH
        )
        copy.start()
        started.append(copy)
        return copy

    def widths(number):
        return RAD if number < STEPS else 1

    def halo_start(number):
        width = widths(number)
        span = width * cols
        here, send, recv = held[number], h_send.at[number], h_recv.at[number]
        copies = [
            push(here.at[pl.ds(0, span)], here.at[pl.ds(own + span, span)], send.at[0], recv.at[0], around[0]),
            push(here.at[pl.ds(own - span, span)], here.at[pl.ds(own, span)], send.at[1], recv.at[1], around[1]),
        ]
        pick = near_pick_ref if number < STEPS else probe_pick_ref
        pack[number][...] = dot(pick[...], here[pl.ds(0, own)]).astype(BF16)
        for k in range(len(SIDES)):
            part = pl.ds(k * PACKET, PACKET)
            copies.append(
                push(pack[number].at[part], got[number].at[part], send.at[2 + k], recv.at[2 + k], around[2 + k])
            )
        return copies

    def halo_end(number, copies):
        for copy in copies:
            copy.wait_recv()
        put = near_put_ref if number < STEPS else probe_put_ref
        base = own + 2 * widths(number) * cols
        held[number][pl.ds(base, put.shape[0])] = dot(put[...], got[number][...]).astype(BF16)

    class Moves:
        def __init__(self, number, source):
            self.number, self.ref, self.source = number, weights[number], source
            half = self.ref.shape[1] // 2
            self.cut = half if half % 16 == 0 else None
            self.slot = {}

        def send(self, slot, src, dst, target):
            self.slot[slot] = push(src, dst, w_send.at[self.number, slot], w_recv.at[self.number, slot], target)

        def go(self, slot, part, target, lo=None, size=None):
            view = self.ref.at[part] if lo is None else self.ref.at[part, pl.ds(lo, size)]
            self.send(slot, view, view, target)

        def begin(self):
            here = self.ref.at[place]
            self.send(0, self.source, here, to_x)
            self.send(1, self.source, here, to_y)
            self.send(2, self.source, here, to_twin)

        def middle(self):
            near_x, near_y = gx * 4 + pa_x, (1 - gx) * 4 + pa
            self.slot[0].wait_recv()
            if self.cut is None:
                self.go(3, near_x, to_y)
            else:
                self.go(3, near_x, to_y, 0, self.cut)
            self.go(5, near_x, to_twin)
            self.slot[1].wait_recv()
            if self.cut is not None:
                self.go(4, near_y, to_x, self.cut, self.cut)
            self.go(6, near_y, to_twin)

        def end(self):
            across = (1 - gx) * 4 + pa_x
            self.slot[3].wait_recv()
            if self.cut is None:
                self.go(7, across, to_twin)
            else:
                self.go(7, across, to_twin, 0, self.cut)
                self.slot[4].wait_recv()
                self.go(8, across, to_twin, self.cut, self.cut)

        def finish(self):
            for slot in (2, 5, 6, 7, 8):
                if slot in self.slot:
                    self.slot[slot].wait_recv()

    tile = 256
    pairs = model // LANES
    keys = kv_s.shape[0]
    half = LANES // 2
    slots = cell_ref.shape[1]
    scale = math.log2(math.e) / math.sqrt(model // HEADS)

    if gather:
        sources = [weight_in[0].at[:, pl.ds(i * model, model)] for i in range(3)] + [weight_in[1], weight_in[2]]
        here_copies = [
            pltpu.make_async_copy(source, weights[i].at[place], w_here.at[i]) for i, source in enumerate(sources)
        ]
        here_copies.append(pltpu.make_async_copy(weight_in[3], head_s, w_here.at[5]))
        move_q, move_k, move_v, move_out, move_query = [Moves(i, source) for i, source in enumerate(sources)]
        move_head = Moves(5, weights[5].at[place])
        for copy in here_copies[::-1]:
            copy.start()
        move_query.begin()
        move_k.begin()
        move_q.begin()
        here_copies[5].wait()
        weights[5][place] = jnp.zeros(weights[5].shape[1:], BF16)
        weights[5][place, 0:CH, 0 : model // ring] = head_s[...]
        move_head.begin()

    for copy in local_copies:
        copy.wait()
    halo = halo_start(0)

    cells = lax.broadcasted_iota(jnp.int32, (own, slots), 0)
    hot_s[...] = jnp.where(cells == cell_ref[...], 1.0, 0.0).astype(BF16)
    quarter = FQ // 4
    freq = lax.broadcasted_iota(jnp.int32, (quarter, slots), 0).astype(F32) + 1.0
    for axis in range(2):
        turns = freq * offset_ref[pl.ds(axis, 1), :]
        sine, cosine = sine_terms(turns - jnp.floor(turns + 0.5))
        feat_s[pl.ds(2 * axis * quarter, quarter)] = sine.astype(BF16)
        feat_s[pl.ds((2 * axis + 1) * quarter, quarter)] = cosine.astype(BF16)
    if gather:
        move_query.middle()
        move_head.middle()
        for copy in here_copies[:5]:
            copy.wait()

    def normalize(number, lo, count):
        part = pl.ds(lo, count)
        values = held[number][part].astype(F32)
        factor = lax.rsqrt(jnp.mean(values * values, axis=-1, keepdims=True) + EPS)
        normed[part] = (values * factor * gain_ref[...].reshape(1, model)).astype(BF16)

    def columns(piece, start, size):
        if gather:
            return weights[piece][:, :, pl.ds(start, size)].reshape(model, size)
        if piece < 3:
            return weight_in[0][:, pl.ds(piece * model + start, size)]
        return weight_in[piece - 2][:, pl.ds(start, size)]

    def project(piece, lo, count):
        def block(i, carry):
            start = pl.multiple_of(i * tile, tile)
            made = dot(normed[pl.ds(lo, count)], columns(piece, start, tile))
            if piece == 0:
                q_s[pl.ds(lo, count), pl.ds(start, tile)] = (made * scale).astype(BF16)
            else:
                kv_s[pl.ds(lo, count), pl.ds((piece - 1) * model + start, tile)] = made.astype(BF16)
            return carry

        lax.fori_loop(0, model // tile, block, 0, unroll=True)

    def attend():
        lane = lax.broadcasted_iota(jnp.int32, (own, LANES), 1)
        low = lane < half
        unit = jnp.where(lane == lax.broadcasted_iota(jnp.int32, (own, LANES), 0), 1.0, 0.0).astype(BF16)
        zero = jnp.zeros((own, LANES), BF16)
        ones = jnp.ones((keys, LANES), BF16)

        def pair(i, carry):
            start = pl.multiple_of(i * LANES, LANES)
            query = q_s[:, pl.ds(start, LANES)]
            both = jnp.concatenate(
                [
                    jnp.concatenate([unit, jnp.where(low, query, zero)], axis=1),
                    jnp.concatenate([unit, jnp.where(low, zero, query)], axis=1),
                ],
                axis=0,
            )
            key = jnp.concatenate([near_bias_ref[...], kv_s[:, pl.ds(start, LANES)]], axis=1)
            scores = dot_t(both, key)
            top = jnp.max(scores, axis=1, keepdims=True)
            weight = jnp.exp2(scores - top).astype(BF16)
            value = jnp.concatenate(
                [kv_s[:, pl.ds(pl.multiple_of(model + start, LANES), LANES)], ones], axis=1
            )
            mixed = dot(weight, value)
            mixed = mixed[:, :LANES] / mixed[:, LANES:]
            att_s[:, pl.ds(start, LANES)] = jnp.where(low, mixed[:own], mixed[own:]).astype(BF16)
            return carry

        lax.fori_loop(0, pairs, pair, 0, unroll=3 if pairs % 3 == 0 else 1)

    def update(step):
        for start in range(0, model, tile):
            cut = pl.ds(start, tile)
            moved = dot(att_s[...], columns(3, start, tile))
            held[step + 1][pl.ds(0, own), cut] = (
                held[step][pl.ds(0, own), cut].astype(F32)
                + moved / STEPS
                + NOISE_COEF * noise_ref[step, :, cut].astype(F32)
            ).astype(BF16)

    halo_end(0, halo)
    normalize(0, 0, keys)
    if gather:
        move_query.end()
        move_head.end()
        move_k.middle()
        move_v.begin()
        move_query.finish()
        move_head.finish()
    turned = weights[4][...].reshape(FQ, model) if gather else weight_in[2][...]
    turned = turned.astype(F32).T.astype(BF16)
    for start in range(0, slots, tile):
        qt_s[:, pl.ds(start, tile)] = (dot(turned, feat_s[:, pl.ds(start, tile)]) * scale).astype(BF16)
    if gather:
        move_q.middle()
        move_k.end()
        move_v.middle()
        move_out.begin()
        move_q.end()
        move_k.finish()
    project(1, 0, keys)
    if gather:
        move_q.finish()
    project(0, 0, own)
    if gather:
        move_v.end()
        move_out.middle()
        move_v.finish()
    project(2, 0, keys)
    attend()
    if gather:
        move_out.end()
        move_out.finish()
    update(0)
    halo = halo_start(1)
    normalize(1, 0, own)
    for piece in range(3):
        project(piece, 0, own)
    halo_end(1, halo)
    normalize(1, own, keys - own)
    project(1, own, keys - own)
    project(2, own, keys - own)
    attend()
    update(1)
    halo = halo_start(2)
    leave = pltpu.make_async_copy(held2.at[pl.ds(0, own)], out_ref, out_sem.at[0])
    leave.start()
    if gather:
        head = jnp.concatenate([weights[5][j, :, 0 : model // ring] for j in range(ring)], axis=1)
    else:
        head = weight_in[3][...]
    every = jnp.concatenate([head.astype(F32)] * HEADS, axis=0)
    line = lax.broadcasted_iota(jnp.int32, every.shape, 0) // 16
    owner = lax.broadcasted_iota(jnp.int32, every.shape, 1) // (model // HEADS)
    every = jnp.where(line == owner, every, 0.0).astype(BF16)

    def decode(lo, count, last):
        part = pl.ds(lo, count)
        turned = dot_t(every, held2[part])
        line = lax.rem(lax.broadcasted_iota(jnp.int32, turned.shape, 0), 16)
        ut_s[:, :, 0:count] = jnp.where(line == CH, 1.0, turned).astype(BF16).reshape(HEADS, 16, count)

        def pair(i, carry):
            start = pl.multiple_of(i * LANES, LANES)
            context = held2[part, pl.ds(start, LANES)]
            bias = probe_bias_ref[part]
            low = lax.broadcasted_iota(jnp.int32, context.shape, 1) < half
            blank = jnp.zeros_like(context)
            key = jnp.concatenate(
                [
                    jnp.concatenate([bias, jnp.where(low, context, blank)], axis=1),
                    jnp.concatenate([bias, jnp.where(low, blank, context)], axis=1),
                ],
                axis=0,
            )
            for first in range(0, slots, tile):
                cut = pl.ds(first, tile)
                scores = dot(key, jnp.concatenate([hot_s[:, cut], qt_s[pl.ds(start, LANES), cut]], axis=0))
                total = val_ref[:, cut] if last else None
                for side in range(2):
                    some = scores[side * count : (side + 1) * count]
                    top = jnp.max(some, axis=0, keepdims=True)
                    weight = jnp.exp2(some - top).astype(BF16)
                    mixed = dot(ut_s[2 * i + side, :, 0:count], weight)[0:8]
                    if not last:
                        place_in = lax.broadcasted_iota(jnp.int32, mixed.shape, 0)
                        part_s[2 * i + side, :, cut] = jnp.where(place_in == CH + 1, top, mixed)
                        continue
                    early = part_s[2 * i + side, :, cut]
                    early_top = early[CH + 1 : CH + 2]
                    both = jnp.maximum(early_top, top)
                    mixed = early * jnp.exp2(early_top - both) + mixed * jnp.exp2(top - both)
                    total = total + mixed / mixed[CH : CH + 1]
                if last:
                    val_ref[:, cut] = total
            return carry

        lax.fori_loop(0, pairs, pair, 0)

    val_ref[...] = jnp.zeros_like(val_ref)
    decode(0, own, False)
    halo_end(2, halo)
    decode(own, held2.shape[0] - own, True)
    leave.wait()
    for copy in started:
        copy.wait_send()


def finish(count_ref, latent_ref, value_ref, out_ref, val_ref, sem):
    copy = pltpu.make_async_copy(latent_ref, out_ref, sem.at[0])
    copy.start()
    slot = lax.broadcasted_iota(jnp.int32, val_ref.shape, 1)
    val_ref[...] = jnp.where(slot < count_ref[0], value_ref[0:CH], 0.0)
    copy.wait()


def local(sizes, latents, noise, proc_gain, w_qkv, w_out, w_query, w_head, probe_cell, probe_offset, probe_count):
    n_gx, n_gy, n_pa = sizes
    rows, cols, model = latents.shape
    own = rows * cols
    slots = probe_cell.shape[0]
    shards = [w_qkv, w_out, w_query, w_head]
    gather = n_gx == 2 and n_pa == 4 and all(shard.shape[0] % 16 == 0 for shard in shards)
    count = n_gx * n_pa
    if not gather:
        shards = [lax.all_gather(shard, ("gx", "pa"), axis=0, tiled=True) for shard in shards]
        shards[3] = jnp.pad(shards[3].T, ((0, 16 - CH), (0, 0)))
    else:
        shards[3] = w_head.T
    near = len(halo_cells(rows, cols, RAD))
    close = len(halo_cells(rows, cols, 1))
    tables = [
        jnp.asarray(table, BF16)
        for table in (
            window_bias(rows, cols, RAD),
            window_bias(rows, cols, 1),
            *packet_tables(rows, cols, RAD),
            *packet_tables(rows, cols, 1),
        )
    ]
    loads = [
        latents.reshape(own, model),
        noise.reshape(STEPS, own, model),
        proc_gain,
        probe_cell.reshape(1, slots),
        probe_offset,
        *tables,
    ]
    scratch = [pltpu.VMEM((near, model), BF16)] + [pltpu.VMEM(load.shape, load.dtype) for load in loads[1:]]
    if gather:
        block = (count, w_out.shape[0], model)
        scratch += [pltpu.VMEM(block, BF16)] * 4
        scratch += [pltpu.VMEM((count,) + w_query.shape, BF16), pltpu.VMEM((count, 16, LANES), BF16)]
        scratch += [pltpu.VMEM(shards[3].shape, BF16)]
        scratch += [pltpu.SemaphoreType.DMA((6, 9)), pltpu.SemaphoreType.DMA((6, 9)), pltpu.SemaphoreType.DMA((6,))]
    scratch += [pltpu.VMEM((size, model), BF16) for size in (near, close)]
    scratch += [pltpu.VMEM((len(SIDES) * PACKET, model), BF16)] * 6
    scratch += [pltpu.SemaphoreType.DMA((STEPS + 1, 8)), pltpu.SemaphoreType.DMA((STEPS + 1, 8))]
    scratch += [pltpu.SemaphoreType.DMA((len(loads),))]
    scratch += [
        pltpu.VMEM((near, model), BF16),
        pltpu.VMEM((own, model), BF16),
        pltpu.VMEM((near, 2 * model), BF16),
        pltpu.VMEM((own, model), BF16),
        pltpu.VMEM((own, slots), BF16),
        pltpu.VMEM((FQ, slots), BF16),
        pltpu.VMEM((model, slots), BF16),
        pltpu.VMEM((HEADS, 16, LANES), BF16),
        pltpu.VMEM((HEADS, 8, slots), F32),
        pltpu.SemaphoreType.DMA((1,)),
    ]
    apart = pl.BlockSpec(memory_space=pltpu.HBM)
    inside = pl.BlockSpec(memory_space=pltpu.VMEM)
    latent_out, values = pl.pallas_call(
        functools.partial(body, (n_gx, n_gy, n_pa, rows, cols, model), gather),
        out_shape=(jax.ShapeDtypeStruct((own, model), BF16), jax.ShapeDtypeStruct((8, slots), F32)),
        in_specs=[apart] * len(loads) + [apart if gather else inside] * len(shards),
        out_specs=[apart, inside],
        scratch_shapes=scratch,
        compiler_params=pltpu.CompilerParams(
            collective_id=0, has_side_effects=True, vmem_limit_bytes=VMEM_BYTES
        ),
        cost_estimate=pl.CostEstimate(flops=6_000_000_000, bytes_accessed=4_000_000, transcendentals=4_000_000),
    )(*loads, *shards)
    latent_out, probe_values = pl.pallas_call(
        finish,
        out_shape=(jax.ShapeDtypeStruct((own, model), BF16), jax.ShapeDtypeStruct((CH, slots), F32)),
        in_specs=[pl.BlockSpec(memory_space=pltpu.SMEM), apart, inside],
        out_specs=[apart, inside],
        scratch_shapes=[pltpu.SemaphoreType.DMA((1,))],
        compiler_params=pltpu.CompilerParams(vmem_limit_bytes=VMEM_BYTES),
    )(probe_count, latent_out, values)
    return (latent_out.reshape(rows, cols, model), probe_values)


def solution(mesh):
    sizes = (mesh.shape["gx"], mesh.shape["gy"], mesh.shape["pa"])
    return jax.shard_map(
        functools.partial(local, sizes),
        mesh=mesh,
        in_specs=(
            P(("gx", "pa"), "gy", None),
            P(None, ("gx", "pa"), "gy", None),
            P(),
            P(("gx", "pa"), None),
            P(("gx", "pa"), None),
            P(("gx", "pa"), None),
            P(("gx", "pa"), None),
            P(("gx", "gy", "pa")),
            P(None, ("gx", "gy", "pa")),
            P(("gx", "gy", "pa")),
        ),
        out_specs=(P(("gx", "pa"), "gy", None), P(None, ("gx", "gy", "pa"))),
        check_vma=False,
    )
```

```python
import functools
import math

import jax
import jax.numpy as jnp
import numpy as np
from jax import lax
from jax.experimental import pallas as pl
from jax.experimental.pallas import tpu as pltpu
from jax.sharding import PartitionSpec as P

HEADS = 12
FQ = 128
CH = 3
RAD = 3
STEPS = 2
EPS = 1e-06
NOISE_COEF = 0.3
MESH = pl.DeviceIdType.MESH
FAR = -1e30
LANES = 128
PACKET = 16
VMEM_BYTES = 61 * 1024 * 1024
SIDES = [(dr, dc) for dc in (-1, 1) for dr in (-1, 0, 1)]
F32 = jnp.float32
BF16 = jnp.bfloat16


def side_rows(rows, width):
    return -(-(rows + 2 * width) * width // 8) * 8


def side_cells(rows, cols, width):
    held = side_rows(rows, width)
    places = []
    for first in (-width, cols):
        group = [(r, first + c) for r in range(-width, rows + width) for c in range(width)]
        places += group + [None] * (held - len(group))
    return places


def halo_cells(rows, cols, width):
    own = [(r, c) for r in range(rows) for c in range(cols)]
    above = [(r, c) for r in range(-width, 0) for c in range(cols)]
    below = [(r, c) for r in range(rows, rows + width) for c in range(cols)]
    return own + above + below + side_cells(rows, cols, width)


def packet_tables(rows, cols, width):
    places = side_cells(rows, cols, width)
    pick = np.zeros((len(SIDES) * PACKET, rows * cols), np.float32)
    put = np.zeros((len(places), len(SIDES) * PACKET), np.float32)
    for number, (dr, dc) in enumerate(SIDES):
        line = number * PACKET
        for place, cell in enumerate(places):
            if cell is None:
                continue
            r, c = cell[0] + dr * rows, cell[1] + dc * cols
            if 0 <= r < rows and 0 <= c < cols:
                pick[line, r * cols + c] = 1.0
                put[place, line] = 1.0
                line += 1
        assert line <= (number + 1) * PACKET
    return pick, put


def window_bias(rows, cols, width):
    cells = halo_cells(rows, cols, width)
    bias = np.full((len(cells), rows * cols), FAR, np.float32)
    for place, cell in enumerate(cells):
        if cell is None:
            continue
        for r in range(rows):
            for c in range(cols):
                if abs(cell[0] - r) <= width and abs(cell[1] - c) <= width:
                    bias[place, r * cols + c] = 0.0
    return bias


def sine_terms(t):
    z = (t * t) * (4.0 * math.pi * math.pi)
    odd = jnp.full_like(t, -1.0 / math.factorial(15))
    for power in range(13, 0, -2):
        odd = odd * z + (-1.0) ** (power // 2) / math.factorial(power)
    even = jnp.full_like(t, 1.0 / math.factorial(16))
    for power in range(14, -1, -2):
        even = even * z + (-1.0) ** (power // 2) / math.factorial(power)
    return odd * (t * (2.0 * math.pi)), even


def dot(a, b):
    return lax.dot_general(a, b, (((1,), (0,)), ((), ())), preferred_element_type=F32)


def dot_t(a, b):
    return lax.dot_general(a, b, (((1,), (1,)), ((), ())), preferred_element_type=F32)


def body(dims, gather, *refs):
    n_gx, n_gy, n_pa, rows, cols, model = dims
    loads, refs = refs[:11], refs[11:]
    weight_in, refs = refs[:4], refs[4:]
    out_ref, val_ref, *refs = refs
    staged, refs = refs[:11], refs[11:]
    (noise_ref, gain_ref, cell_ref, offset_ref, near_bias_ref, probe_bias_ref, near_pick_ref, near_put_ref,
     probe_pick_ref, probe_put_ref) = staged[1:]
    held0 = staged[0]
    if gather:
        weights, refs = refs[:6], refs[6:]
        head_s, w_send, w_recv, w_here, *refs = refs
    (held1, held2, got0, got1, got2, pack0, pack1, pack2, h_send, h_recv, l_sem, normed, q_s, kv_s, att_s,
     hot_s, feat_s, qt_s, ut_s, part_s, out_sem) = refs
    held, got, pack = (held0, held1, held2), (got0, got1, got2), (pack0, pack1, pack2)
    own = rows * cols
    gx, gy, pa = lax.axis_index("gx"), lax.axis_index("gy"), lax.axis_index("pa")
    ring = n_gx * n_pa
    place = gx * n_pa + pa

    local_copies = []
    for number, source in enumerate(loads):
        target = held0.at[pl.ds(0, own)] if number == 0 else staged[number]
        local_copies.append(pltpu.make_async_copy(source, target, l_sem.at[number]))
        local_copies[-1].start()

    def device(dr, dc):
        r = lax.rem(place + dr + ring, ring)
        return (lax.div(r, n_pa), lax.rem(gy + dc + n_gy, n_gy), lax.rem(r, n_pa))

    around = [device(-1, 0), device(1, 0)] + [device(dr, dc) for dr, dc in SIDES]
    partners = list(around)
    if gather:
        pa_x = lax.rem(pa + 2, 4)
        to_x, to_y = (gx, gy, pa_x), (1 - gx, gy, pa)
        to_twin = (gx, gy, pa + 1 - 2 * lax.rem(pa, 2))
        partners += [to_x, to_y, to_twin]
    barrier = pltpu.get_barrier_semaphore()
    for target in partners:
        pl.semaphore_signal(barrier, inc=1, device_id=target, device_id_type=MESH)
    pl.semaphore_wait(barrier, len(partners))

    started = []

    def push(src, dst, send, recv, target):
        copy = pltpu.make_async_remote_copy(
            src_ref=src, dst_ref=dst, send_sem=send, recv_sem=recv, device_id=target, device_id_type=MESH
        )
        copy.start()
        started.append(copy)
        return copy

    def widths(number):
        return RAD if number < STEPS else 1

    def halo_start(number):
        width = widths(number)
        span = width * cols
        here, send, recv = held[number], h_send.at[number], h_recv.at[number]
        copies = [
            push(here.at[pl.ds(0, span)], here.at[pl.ds(own + span, span)], send.at[0], recv.at[0], around[0]),
            push(here.at[pl.ds(own - span, span)], here.at[pl.ds(own, span)], send.at[1], recv.at[1], around[1]),
        ]
        pick = near_pick_ref if number < STEPS else probe_pick_ref
        pack[number][...] = dot(pick[...], here[pl.ds(0, own)]).astype(BF16)
        for k in range(len(SIDES)):
            part = pl.ds(k * PACKET, PACKET)
            copies.append(
                push(pack[number].at[part], got[number].at[part], send.at[2 + k], recv.at[2 + k], around[2 + k])
            )
        return copies

    def halo_end(number, copies):
        for copy in copies:
            copy.wait_recv()
        put = near_put_ref if number < STEPS else probe_put_ref
        base = own + 2 * widths(number) * cols
        held[number][pl.ds(base, put.shape[0])] = dot(put[...], got[number][...]).astype(BF16)

    class Moves:
        def __init__(self, number, source):
            self.number, self.ref, self.source = number, weights[number], source
            half = self.ref.shape[1] // 2
            self.cut = half if half % 16 == 0 else None
            self.slot = {}

        def send(self, slot, src, dst, target):
            self.slot[slot] = push(src, dst, w_send.at[self.number, slot], w_recv.at[self.number, slot], target)

        def go(self, slot, part, target, lo=None, size=None):
            view = self.ref.at[part] if lo is None else self.ref.at[part, pl.ds(lo, size)]
            self.send(slot, view, view, target)

        def begin(self):
            here = self.ref.at[place]
            self.send(0, self.source, here, to_x)
            self.send(1, self.source, here, to_y)
            self.send(2, self.source, here, to_twin)

        def middle(self):
            near_x, near_y = gx * 4 + pa_x, (1 - gx) * 4 + pa
            self.slot[0].wait_recv()
            if self.cut is None:
                self.go(3, near_x, to_y)
            else:
                self.go(3, near_x, to_y, 0, self.cut)
            self.go(5, near_x, to_twin)
            self.slot[1].wait_recv()
            if self.cut is not None:
                self.go(4, near_y, to_x, self.cut, self.cut)
            self.go(6, near_y, to_twin)

        def end(self):
            across = (1 - gx) * 4 + pa_x
            self.slot[3].wait_recv()
            if self.cut is None:
                self.go(7, across, to_twin)
            else:
                self.go(7, across, to_twin, 0, self.cut)
                self.slot[4].wait_recv()
                self.go(8, across, to_twin, self.cut, self.cut)

        def finish(self):
            for slot in (2, 5, 6, 7, 8):
                if slot in self.slot:
                    self.slot[slot].wait_recv()

    tile = 256
    pairs = model // LANES
    keys = kv_s.shape[0]
    half = LANES // 2
    slots = cell_ref.shape[1]
    scale = math.log2(math.e) / math.sqrt(model // HEADS)

    if gather:
        sources = [weight_in[0].at[:, pl.ds(i * model, model)] for i in range(3)] + [weight_in[1], weight_in[2]]
        here_copies = [
            pltpu.make_async_copy(source, weights[i].at[place], w_here.at[i]) for i, source in enumerate(sources)
        ]
        here_copies.append(pltpu.make_async_copy(weight_in[3], head_s, w_here.at[5]))
        move_q, move_k, move_v, move_out, move_query = [Moves(i, source) for i, source in enumerate(sources)]
        move_head = Moves(5, weights[5].at[place])
        for copy in here_copies[::-1]:
            copy.start()
        move_query.begin()
        move_k.begin()
        move_q.begin()
        here_copies[5].wait()
        weights[5][place] = jnp.zeros(weights[5].shape[1:], BF16)
        weights[5][place, 0:CH, 0 : model // ring] = head_s[...]
        move_head.begin()

    for copy in local_copies:
        copy.wait()
    halo = halo_start(0)

    cells = lax.broadcasted_iota(jnp.int32, (own, slots), 0)
    hot_s[...] = jnp.where(cells == cell_ref[...], 1.0, 0.0).astype(BF16)
    quarter = FQ // 4
    freq = lax.broadcasted_iota(jnp.int32, (quarter, slots), 0).astype(F32) + 1.0
    for axis in range(2):
        turns = freq * offset_ref[pl.ds(axis, 1), :]
        sine, cosine = sine_terms(turns - jnp.floor(turns + 0.5))
        feat_s[pl.ds(2 * axis * quarter, quarter)] = sine.astype(BF16)
        feat_s[pl.ds((2 * axis + 1) * quarter, quarter)] = cosine.astype(BF16)
    if gather:
        move_query.middle()
        move_head.middle()
        for copy in here_copies[:5]:
            copy.wait()

    def normalize(number, lo, count):
        part = pl.ds(lo, count)
        values = held[number][part].astype(F32)
        factor = lax.rsqrt(jnp.mean(values * values, axis=-1, keepdims=True) + EPS)
        normed[part] = (values * factor * gain_ref[...].reshape(1, model)).astype(BF16)

    def columns(piece, start, size):
        if gather:
            return weights[piece][:, :, pl.ds(start, size)].reshape(model, size)
        if piece < 3:
            return weight_in[0][:, pl.ds(piece * model + start, size)]
        return weight_in[piece - 2][:, pl.ds(start, size)]

    def project(piece, lo, count):
        def block(i, carry):
            start = pl.multiple_of(i * tile, tile)
            made = dot(normed[pl.ds(lo, count)], columns(piece, start, tile))
            if piece == 0:
                q_s[pl.ds(lo, count), pl.ds(start, tile)] = (made * scale).astype(BF16)
            else:
                kv_s[pl.ds(lo, count), pl.ds((piece - 1) * model + start, tile)] = made.astype(BF16)
            return carry

        lax.fori_loop(0, model // tile, block, 0, unroll=True)

    def attend():
        lane = lax.broadcasted_iota(jnp.int32, (own, LANES), 1)
        low = lane < half
        unit = jnp.where(lane == lax.broadcasted_iota(jnp.int32, (own, LANES), 0), 1.0, 0.0).astype(BF16)
        zero = jnp.zeros((own, LANES), BF16)
        ones = jnp.ones((keys, LANES), BF16)

        def pair(i, carry):
            start = pl.multiple_of(i * LANES, LANES)
            query = q_s[:, pl.ds(start, LANES)]
            both = jnp.concatenate(
                [
                    jnp.concatenate([unit, jnp.where(low, query, zero)], axis=1),
                    jnp.concatenate([unit, jnp.where(low, zero, query)], axis=1),
                ],
                axis=0,
            )
            key = jnp.concatenate([near_bias_ref[...], kv_s[:, pl.ds(start, LANES)]], axis=1)
            scores = dot_t(both, key)
            top = jnp.max(scores, axis=1, keepdims=True)
            weight = jnp.exp2(scores - top).astype(BF16)
            value = jnp.concatenate(
                [kv_s[:, pl.ds(pl.multiple_of(model + start, LANES), LANES)], ones], axis=1
            )
            mixed = dot(weight, value)
            mixed = mixed[:, :LANES] / mixed[:, LANES:]
            att_s[:, pl.ds(start, LANES)] = jnp.where(low, mixed[:own], mixed[own:]).astype(BF16)
            return carry

        lax.fori_loop(0, pairs, pair, 0, unroll=3 if pairs % 3 == 0 else 1)

    def update(step):
        for start in range(0, model, tile):
            cut = pl.ds(start, tile)
            moved = dot(att_s[...], columns(3, start, tile))
            held[step + 1][pl.ds(0, own), cut] = (
                held[step][pl.ds(0, own), cut].astype(F32)
                + moved / STEPS
                + NOISE_COEF * noise_ref[step, :, cut].astype(F32)
            ).astype(BF16)

    halo_end(0, halo)
    normalize(0, 0, keys)
    if gather:
        move_query.end()
        move_head.end()
        move_k.middle()
        move_v.begin()
        move_query.finish()
        move_head.finish()
    turned = weights[4][...].reshape(FQ, model) if gather else weight_in[2][...]
    turned = turned.astype(F32).T.astype(BF16)
    for start in range(0, slots, tile):
        qt_s[:, pl.ds(start, tile)] = (dot(turned, feat_s[:, pl.ds(start, tile)]) * scale).astype(BF16)
    if gather:
        move_q.middle()
        move_k.end()
        move_v.middle()
        move_out.begin()
        move_q.end()
        move_k.finish()
    project(1, 0, keys)
    if gather:
        move_q.finish()
    project(0, 0, own)
    if gather:
        move_v.end()
        move_out.middle()
        move_v.finish()
    project(2, 0, keys)
    attend()
    if gather:
        move_out.end()
        move_out.finish()
    update(0)
    halo = halo_start(1)
    normalize(1, 0, own)
    for piece in range(3):
        project(piece, 0, own)
    halo_end(1, halo)
    normalize(1, own, keys - own)
    project(1, own, keys - own)
    project(2, own, keys - own)
    attend()
    update(1)
    halo = halo_start(2)
    leave = pltpu.make_async_copy(held2.at[pl.ds(0, own)], out_ref, out_sem.at[0])
    leave.start()
    if gather:
        head = jnp.concatenate([weights[5][j, :, 0 : model // ring] for j in range(ring)], axis=1)
    else:
        head = weight_in[3][...]
    every = jnp.concatenate([head.astype(F32)] * HEADS, axis=0)
    line = lax.broadcasted_iota(jnp.int32, every.shape, 0) // 16
    owner = lax.broadcasted_iota(jnp.int32, every.shape, 1) // (model // HEADS)
    every = jnp.where(line == owner, every, 0.0).astype(BF16)

    def decode(lo, count, last):
        part = pl.ds(lo, count)
        turned = dot_t(every, held2[part])
        line = lax.rem(lax.broadcasted_iota(jnp.int32, turned.shape, 0), 16)
        ut_s[:, :, 0:count] = jnp.where(line == CH, 1.0, turned).astype(BF16).reshape(HEADS, 16, count)

        def pair(i, carry):
            start = pl.multiple_of(i * LANES, LANES)
            context = held2[part, pl.ds(start, LANES)]
            bias = probe_bias_ref[part]
            low = lax.broadcasted_iota(jnp.int32, context.shape, 1) < half
            blank = jnp.zeros_like(context)
            key = jnp.concatenate(
                [
                    jnp.concatenate([bias, jnp.where(low, context, blank)], axis=1),
                    jnp.concatenate([bias, jnp.where(low, blank, context)], axis=1),
                ],
                axis=0,
            )
            for first in range(0, slots, tile):
                cut = pl.ds(first, tile)
                scores = dot(key, jnp.concatenate([hot_s[:, cut], qt_s[pl.ds(start, LANES), cut]], axis=0))
                total = val_ref[:, cut] if last else None
                for side in range(2):
                    some = scores[side * count : (side + 1) * count]
                    top = jnp.max(some, axis=0, keepdims=True)
                    weight = jnp.exp2(some - top).astype(BF16)
                    mixed = dot(ut_s[2 * i + side, :, 0:count], weight)[0:8]
                    if not last:
                        place_in = lax.broadcasted_iota(jnp.int32, mixed.shape, 0)
                        part_s[2 * i + side, :, cut] = jnp.where(place_in == CH + 1, top, mixed)
                        continue
                    early = part_s[2 * i + side, :, cut]
                    early_top = early[CH + 1 : CH + 2]
                    both = jnp.maximum(early_top, top)
                    mixed = early * jnp.exp2(early_top - both) + mixed * jnp.exp2(top - both)
                    total = total + mixed / mixed[CH : CH + 1]
                if last:
                    val_ref[:, cut] = total
            return carry

        lax.fori_loop(0, pairs, pair, 0)

    val_ref[...] = jnp.zeros_like(val_ref)
    decode(0, own, False)
    halo_end(2, halo)
    decode(own, held2.shape[0] - own, True)
    leave.wait()
    for copy in started:
        copy.wait_send()


def finish(count_ref, latent_ref, value_ref, out_ref, val_ref):
    out_ref[...] = latent_ref[...]
    slot = lax.broadcasted_iota(jnp.int32, val_ref.shape, 1)
    val_ref[...] = jnp.where(slot < count_ref[0], value_ref[0:CH], 0.0)


def local(sizes, latents, noise, proc_gain, w_qkv, w_out, w_query, w_head, probe_cell, probe_offset, probe_count):
    n_gx, n_gy, n_pa = sizes
    rows, cols, model = latents.shape
    own = rows * cols
    slots = probe_cell.shape[0]
    shards = [w_qkv, w_out, w_query, w_head]
    gather = n_gx == 2 and n_pa == 4 and all(shard.shape[0] % 16 == 0 for shard in shards)
    count = n_gx * n_pa
    if not gather:
        shards = [lax.all_gather(shard, ("gx", "pa"), axis=0, tiled=True) for shard in shards]
        shards[3] = jnp.pad(shards[3].T, ((0, 16 - CH), (0, 0)))
    else:
        shards[3] = w_head.T
    near = len(halo_cells(rows, cols, RAD))
    close = len(halo_cells(rows, cols, 1))
    tables = [
        jnp.asarray(table, BF16)
        for table in (
            window_bias(rows, cols, RAD),
            window_bias(rows, cols, 1),
            *packet_tables(rows, cols, RAD),
            *packet_tables(rows, cols, 1),
        )
    ]
    loads = [
        latents.reshape(own, model),
        noise.reshape(STEPS, own, model),
        proc_gain,
        probe_cell.reshape(1, slots),
        probe_offset,
        *tables,
    ]
    scratch = [pltpu.VMEM((near, model), BF16)] + [pltpu.VMEM(load.shape, load.dtype) for load in loads[1:]]
    if gather:
        block = (count, w_out.shape[0], model)
        scratch += [pltpu.VMEM(block, BF16)] * 4
        scratch += [pltpu.VMEM((count,) + w_query.shape, BF16), pltpu.VMEM((count, 16, LANES), BF16)]
        scratch += [pltpu.VMEM(shards[3].shape, BF16)]
        scratch += [pltpu.SemaphoreType.DMA((6, 9)), pltpu.SemaphoreType.DMA((6, 9)), pltpu.SemaphoreType.DMA((6,))]
    scratch += [pltpu.VMEM((size, model), BF16) for size in (near, close)]
    scratch += [pltpu.VMEM((len(SIDES) * PACKET, model), BF16)] * 6
    scratch += [pltpu.SemaphoreType.DMA((STEPS + 1, 8)), pltpu.SemaphoreType.DMA((STEPS + 1, 8))]
    scratch += [pltpu.SemaphoreType.DMA((len(loads),))]
    scratch += [
        pltpu.VMEM((near, model), BF16),
        pltpu.VMEM((own, model), BF16),
        pltpu.VMEM((near, 2 * model), BF16),
        pltpu.VMEM((own, model), BF16),
        pltpu.VMEM((own, slots), BF16),
        pltpu.VMEM((FQ, slots), BF16),
        pltpu.VMEM((model, slots), BF16),
        pltpu.VMEM((HEADS, 16, LANES), BF16),
        pltpu.VMEM((HEADS, 8, slots), F32),
        pltpu.SemaphoreType.DMA((1,)),
    ]
    apart = pl.BlockSpec(memory_space=pltpu.HBM)
    inside = pl.BlockSpec(memory_space=pltpu.VMEM)
    latent_out, values = pl.pallas_call(
        functools.partial(body, (n_gx, n_gy, n_pa, rows, cols, model), gather),
        out_shape=(jax.ShapeDtypeStruct((own, model), BF16), jax.ShapeDtypeStruct((8, slots), F32)),
        in_specs=[apart] * len(loads) + [apart if gather else inside] * len(shards),
        out_specs=[apart, inside],
        scratch_shapes=scratch,
        compiler_params=pltpu.CompilerParams(
            collective_id=0, has_side_effects=True, vmem_limit_bytes=VMEM_BYTES
        ),
        cost_estimate=pl.CostEstimate(flops=6_000_000_000, bytes_accessed=4_000_000, transcendentals=4_000_000),
    )(*loads, *shards)
    latent_out, probe_values = pl.pallas_call(
        finish,
        out_shape=(jax.ShapeDtypeStruct((own, model), BF16), jax.ShapeDtypeStruct((CH, slots), F32)),
        in_specs=[pl.BlockSpec(memory_space=pltpu.SMEM), inside, inside],
        out_specs=[inside, inside],
        compiler_params=pltpu.CompilerParams(vmem_limit_bytes=VMEM_BYTES),
    )(probe_count, latent_out, values)
    return (latent_out.reshape(rows, cols, model), probe_values)


def solution(mesh):
    sizes = (mesh.shape["gx"], mesh.shape["gy"], mesh.shape["pa"])
    return jax.shard_map(
        functools.partial(local, sizes),
        mesh=mesh,
        in_specs=(
            P(("gx", "pa"), "gy", None),
            P(None, ("gx", "pa"), "gy", None),
            P(),
            P(("gx", "pa"), None),
            P(("gx", "pa"), None),
            P(("gx", "pa"), None),
            P(("gx", "pa"), None),
            P(("gx", "gy", "pa")),
            P(None, ("gx", "gy", "pa")),
            P(("gx", "gy", "pa")),
        ),
        out_specs=(P(("gx", "pa"), "gy", None), P(None, ("gx", "gy", "pa"))),
        check_vma=False,
    )
```
